128 devices in a mesh: req: 8 (over x, core), exp: 16 (over y, z).
Axes of the slice: x: 4, y: 4, z: 4, core: 2. Of those that a mesh axis runs over, the one named last changes fastest.
Arguments:
- latent_cache: bfloat16 [1024, 1024, 576], P(('req', 'exp')), may hold values from -6 to 6
- context_lengths: int32 [1024], P(('req', 'exp')), may hold values from 2 to 1022, as said below
- destination: int32 [1024], P(('req', 'exp')), may hold values from 0 to 1023, as said below
- query_first: bfloat16 [1024, 128, 576], P(('req', 'exp')), may hold values from -240 to 240
- latent_first: bfloat16 [1024, 576], P(('req', 'exp')), may hold values from -6 to 6
- query_second: bfloat16 [1024, 128, 576], P(('req', 'exp')), may hold values from -240 to 240
- latent_second: bfloat16 [1024, 576], P(('req', 'exp')), may hold values from -6 to 6
- hidden: bfloat16 [1024, 7168], P(('req', 'exp')), may hold values from -6 to 6
- expert_ids: int32 [1024, 4], P(('req', 'exp')), may hold values from 0 to 15, all different within a row; in each aligned block of 8 rows (0 to 7, 8 to 15, ...) at most 4 rows name the same one
- gate_weights: float32 [1024, 4], P(('req', 'exp')), may hold values from 0.1 to 1
- expert_gate: bfloat16 [16, 7168, 2048], P('exp', None, 'req'), may hold values from -0.0625 to 0.0625
- expert_up: bfloat16 [16, 7168, 2048], P('exp', None, 'req'), may hold values from -0.0625 to 0.0625
- expert_down: bfloat16 [16, 2048, 7168], P('exp', 'req'), may hold values from -0.125 to 0.125
Outputs:
- context_first: bfloat16 [1024, 128, 512], P(('req', 'exp'))
- context_second: bfloat16 [1024, 128, 512], P(('req', 'exp'))
- routed_output: bfloat16 [1024, 7168], P(('req', 'exp'))
The draws below stay inside these ranges and needn't reach their ends.
Inputs may be any that keep to these rules, and one draw needn't show every extreme that they name: Request g sits on device g // 8 (devices in the order req, then exp) in slot g % 8. destination is a permutation that keeps every request in its exp column; on each device exactly two requests go to two different other ranks of req and exactly those two slots receive one request each from two different other ranks; all other requests keep their slot. `context_lengths`: at least 2; some request has exactly 1022. `expert_ids`: in the rows of one device no expert is named more than 4 times, and on some device some expert is named exactly 4 times.
All inputs are finite; a program needn't handle non-finite values.
Results may differ from the reference program's by a relative error of at most 0.015.
Values may be sent and summed in bfloat16 or wider, within the bound.
A program may use at most 192 MiB of HBM per device.

```python
import math
import jax
import jax.numpy as jnp
import numpy as np
from jax import lax

D = 7168
HEADS = 128
LATENT = 512
ROPE = 64
FF = 2048
REQ_DEV = 8
CONTEXT = 1024
TOPK = 4
KV_WIDTH = 576
EXPERTS = 16
REQUESTS = 1024
CAPACITY = 4
N_REQ = 8
N_EXP = 16
DEVICES = 128


def anchor_rows(key):
    values = jax.random.normal(jax.random.fold_in(key, 5), (REQUESTS, ROPE), jnp.float32)
    return jnp.clip(values, -4.0, 4.0)


def migration_table(key):
    key = jax.random.fold_in(key, 7)
    order_key, first_key, offset_key, slot_key = jax.random.split(key, 4)
    rank_order = jax.vmap(lambda sub_key: jax.random.permutation(sub_key, N_REQ))(jax.random.split(order_key, N_EXP)).astype(jnp.int32)
    first_shift = jax.random.randint(first_key, (N_EXP,), 1, N_REQ, dtype=jnp.int32)
    second_shift = 1 + (first_shift - 1 + jax.random.randint(offset_key, (N_EXP,), 1, N_REQ - 1, dtype=jnp.int32)) % (N_REQ - 1)
    picked_slots = jax.vmap(lambda sub_key: jax.random.permutation(sub_key, REQ_DEV)[:2])(jax.random.split(slot_key, N_EXP * N_REQ))
    picked_slots = picked_slots.reshape(N_EXP, N_REQ, 2).astype(jnp.int32)
    column_ids = jnp.broadcast_to(jnp.arange(N_EXP, dtype=jnp.int32)[:, None], (N_EXP, N_REQ))
    spots_now = jnp.broadcast_to(jnp.arange(N_REQ, dtype=jnp.int32)[None, :], (N_EXP, N_REQ))
    destination_table = jnp.arange(REQUESTS, dtype=jnp.int32).reshape(N_REQ, N_EXP, REQ_DEV)
    for member_pick, shift_amount in ((0, first_shift), (1, second_shift)):
        target_spot = (spots_now + shift_amount[:, None]) % N_REQ
        target_rank = jnp.take_along_axis(rank_order, target_spot, axis=1)
        source_slot = picked_slots[:, :, member_pick]
        target_slot = jnp.take_along_axis(picked_slots[:, :, member_pick], target_spot, axis=1)
        new_index = (target_rank * N_EXP + column_ids) * REQ_DEV + target_slot
        destination_table = destination_table.at[rank_order, column_ids, source_slot].set(new_index)
    return destination_table.reshape(REQUESTS).astype(jnp.int32)


def draw_destination(key, part):
    return migration_table(key)


def draw_context_lengths(key, part):
    key = jax.random.fold_in(key, 11)
    ceiling_key, length_key, row_key = jax.random.split(key, 3)
    ceiling = jax.random.randint(ceiling_key, (DEVICES, 1), CONTEXT // 4, CONTEXT - 1, dtype=jnp.int32)
    lengths = jax.random.randint(length_key, (DEVICES, REQ_DEV), 2, ceiling, dtype=jnp.int32)
    chosen_row = jax.random.randint(row_key, (), 0, REQUESTS, dtype=jnp.int32)
    return lengths.reshape(REQUESTS).at[chosen_row].set(CONTEXT - 2).astype(jnp.int32)


def draw_latent_cache(key, part):
    anchor = anchor_rows(key)
    key = jax.random.fold_in(key, 13)
    cache_values = jnp.clip(jax.random.normal(key, (REQUESTS, CONTEXT, KV_WIDTH), jnp.float32), -6.0, 6.0)
    cache_values = cache_values.at[:, 0, LATENT:].set(anchor)
    return cache_values.astype(jnp.bfloat16)


def draw_query_first(key, part):
    key = jax.random.fold_in(key, 17)
    base_key = jax.random.fold_in(key, 0)
    base_values = jax.random.normal(base_key, (REQUESTS, HEADS, KV_WIDTH), jnp.float32)
    return base_values.astype(jnp.bfloat16)


def draw_query_second(key, part):
    key = jax.random.fold_in(key, 19)
    base_key = jax.random.fold_in(key, 0)
    base_values = jax.random.normal(base_key, (REQUESTS, HEADS, KV_WIDTH), jnp.float32)
    return base_values.astype(jnp.bfloat16)


def block_levels(rng, extent, pieces, smallest, top_value):
    factor_of, own = 1.0, jax.random.fold_in(rng, 6)
    for axis_at, blocks in pieces:
        steps = jnp.exp(jax.random.uniform(jax.random.fold_in(own, axis_at), (blocks,), jnp.float32, smallest / len(pieces), top_value / len(pieces)))
        factor_of = factor_of * jnp.repeat(steps, extent[axis_at] // blocks).reshape([-1 if axis == axis_at else 1 for axis in range(len(extent))])
    return factor_of


def shared_out(rng, own, number, rows, count, top, most, skew):
    sequence = jax.random.permutation(rng, count)
    heavy_load, usual = load_shares(count, rows * top, most, skew, True), load_shares(count, rows * top, most, skew, False)
    places = jnp.arange(count)

    def named(sizes, rotation):
        used = int((sizes > 0).sum())
        fixed = max(1, used // 4)
        shifted = fixed + (places - fixed + rotation * (used - fixed)) % max(1, count - fixed)
        return jnp.zeros((count,), jnp.int32).at[sequence[jnp.where(places < fixed, places, shifted)]].set(jnp.asarray(sizes, jnp.int32))

    sizes = jnp.where(number % 4 == 0, named(heavy_load, number // 4), named(usual, number - number // 4 - 1))
    mixed = jax.random.permutation(jax.random.fold_in(own, 3), count)
    source_of, taker = mixed[0:count // 2 * 2:2], mixed[1:count // 2 * 2:2]
    slack = jnp.minimum(sizes[source_of] - 1, most - sizes[taker]) // 2
    slack = jnp.where((source_of == sequence[0]) | (taker == sequence[0]) | (sizes[taker] == 0), 0, jnp.maximum(slack, 0))
    shifted = jax.random.randint(jax.random.fold_in(own, 4), (count // 2,), 0, 1 << 20) % (slack + 1)
    sizes = sizes.at[source_of].add(-shifted).at[taker].add(shifted)
    items = jnp.searchsorted(jnp.cumsum(sizes), jnp.arange(rows * top), side="right").astype(jnp.int32)
    listing = items.reshape(top, rows).T
    listing = listing[jax.random.permutation(jax.random.fold_in(own, 1), rows)]
    rotation = jax.random.randint(jax.random.fold_in(own, 2), (rows, 1), 0, top)
    return jnp.take_along_axis(listing, (jnp.arange(top)[None, :] + rotation) % top, axis=1)


def load_shares(number_of, total, reach, lean, full):
    loads = [(1 << 20) // math.isqrt(standing ** lean) + 1 for standing in range(1, number_of + 1)]
    largest = reach if full else min(reach, max(-(-total // number_of), total * loads[0] // sum(loads)))
    least = 1 if total - largest >= number_of - 1 else 0
    counts, surplus = [largest] + [least] * (number_of - 1), total - largest - least * (number_of - 1)
    while surplus > 0:
        candidates = [i for i in range(1, number_of) if counts[i] < largest] or [i for i in range(1, number_of) if counts[i] < reach]
        mass, remaining = sum([loads[i] for i in candidates]), surplus
        for i in candidates:
            more = min(reach - counts[i], max(1, remaining * loads[i] // mass), surplus)
            counts[i] = counts[i] + more
            surplus = surplus - more
    return np.array(counts)


def gaussian(stream_key, dims, width, reach, pieces=(), kind=jnp.bfloat16):
    loudness = block_levels(stream_key, dims, pieces, -0.22, 0.18) if pieces else 1.0
    values = jax.random.normal(stream_key, dims, jnp.float32) * width * loudness
    return jnp.minimum(jnp.maximum(values, -reach), reach).astype(kind)


def setup_inputs(seed: int = 0) -> dict:
    seeds = jax.random.split(jax.random.key(seed), 14)
    latent_cache = draw_latent_cache(jax.random.fold_in(seeds[13], 71), 0)
    context_lengths = draw_context_lengths(jax.random.fold_in(seeds[13], 71), 0)
    destination = draw_destination(jax.random.fold_in(seeds[13], 71), 0)
    query_first = draw_query_first(jax.random.fold_in(seeds[13], 71), 0)
    latent_first = gaussian(seeds[4], (REQUESTS, KV_WIDTH), 1.0, 6.0, ((0, 128),))
    query_second = draw_query_second(jax.random.fold_in(seeds[13], 71), 0)
    latent_second = gaussian(seeds[6], (REQUESTS, KV_WIDTH), 1.0, 6.0, ((0, 128),))
    hidden = gaussian(seeds[7], (REQUESTS, D), 1.0, 6.0, ((0, 128),))
    expert_ids_keys = jax.random.split(jax.random.fold_in(seeds[8], 1), REQUESTS // REQ_DEV)
    expert_ids_turns = jax.random.permutation(jax.random.fold_in(seeds[8], 3), REQUESTS // REQ_DEV)
    expert_ids = jax.vmap(lambda own, number: shared_out(jax.random.fold_in(seeds[8], 2), own, number, REQ_DEV, EXPERTS, TOPK, CAPACITY, 1))(expert_ids_keys, expert_ids_turns).reshape((REQUESTS, TOPK))
    gate_weights = jnp.clip(jnp.exp(math.log(1.0) - 2.3025851 * jax.random.uniform(seeds[9], (REQUESTS, TOPK), jnp.float32) ** block_levels(seeds[9], (REQUESTS, TOPK), ((0, 128),), -0.2, 0.2)), 0.1, 1.0)
    expert_gate = gaussian(seeds[10], (EXPERTS, D, FF), D ** -0.5, 0.0625, ((0, 16), (2, 8)))
    expert_up = gaussian(seeds[11], (EXPERTS, D, FF), D ** -0.5, 0.0625, ((0, 16), (2, 8)))
    expert_down = gaussian(seeds[12], (EXPERTS, FF, D), FF ** -0.5, 0.125, ((0, 16), (1, 8)))
    return {"latent_cache": latent_cache, "context_lengths": context_lengths, "destination": destination, "query_first": query_first, "latent_first": latent_first, "query_second": query_second, "latent_second": latent_second, "hidden": hidden, "expert_ids": expert_ids, "gate_weights": gate_weights, "expert_gate": expert_gate, "expert_up": expert_up, "expert_down": expert_down}


score_scale = 1.0 / math.sqrt(192.0)

def attention(query_rows, key_rows, limit):
    scores = jnp.dot(query_rows, key_rows.T, preferred_element_type=jnp.float32) * score_scale
    positions = jnp.arange(CONTEXT, dtype=jnp.int32)
    scores = jnp.where(positions[None, :] <= limit, scores, -jnp.inf)
    highest = lax.optimization_barrier(jnp.max(scores, axis=1, keepdims=True))
    weights = jnp.exp(scores - highest)
    probs_bf = (weights / lax.optimization_barrier(jnp.sum(weights, axis=1, keepdims=True))).astype(jnp.bfloat16)
    return jnp.dot(probs_bf, key_rows[:, :LATENT], preferred_element_type=jnp.float32).astype(jnp.bfloat16)

def put_row(key_rows, new_row, position):
    return lax.dynamic_update_slice(key_rows, new_row[None, :], (position.astype(jnp.int32), jnp.zeros((), jnp.int32)))

def expert_rows(token_rows, gate_matrix, up_matrix, down_matrix):
    gate_act = jnp.dot(token_rows, gate_matrix, preferred_element_type=jnp.float32)
    up_act = jnp.dot(token_rows, up_matrix, preferred_element_type=jnp.float32)
    inner_act = (jax.nn.silu(gate_act) * up_act).astype(jnp.bfloat16)
    split_inner = inner_act.reshape(token_rows.shape[0], N_REQ, FF // N_REQ).astype(jnp.float32)
    split_down = down_matrix.reshape(N_REQ, FF // N_REQ, D).astype(jnp.float32)
    partial_out = jnp.einsum('sri,rid->rsd', split_inner, split_down, precision=lax.Precision.HIGHEST).astype(jnp.bfloat16)
    return lax.optimization_barrier(jnp.sum(partial_out.astype(jnp.float32), axis=0))

def reference(latent_cache, context_lengths, destination, query_first, latent_first, query_second, latent_second, hidden, expert_ids, gate_weights, expert_gate, expert_up, expert_down):

    def first_step(request_index):
        key_rows = put_row(latent_cache[request_index], latent_first[request_index], context_lengths[request_index])
        return attention(query_first[request_index], key_rows, context_lengths[request_index])
    context_first = lax.map(first_step, jnp.arange(REQUESTS, dtype=jnp.int32))
    root = jnp.zeros((REQUESTS,), jnp.int32).at[destination].set(jnp.arange(REQUESTS, dtype=jnp.int32))

    def second_step(request_index):
        source = root[request_index]
        length = context_lengths[source]
        key_rows = put_row(latent_cache[source], latent_first[source], length)
        key_rows = put_row(key_rows, latent_second[request_index], length + 1)
        return attention(query_second[request_index], key_rows, length + 1)
    context_second = lax.map(second_step, jnp.arange(REQUESTS, dtype=jnp.int32))
    flat_ids = expert_ids.reshape(DEVICES, REQ_DEV * TOPK)
    onehot = (flat_ids[:, :, None] == jnp.arange(EXPERTS, dtype=jnp.int32)[None, None, :]).astype(jnp.int32)
    position = lax.optimization_barrier(jnp.sum((jnp.cumsum(onehot, axis=1) - onehot) * onehot, axis=2)).astype(jnp.int32)
    device_ids = jnp.broadcast_to(jnp.arange(DEVICES, dtype=jnp.int32)[:, None], flat_ids.shape)
    token_ids = (device_ids * REQ_DEV + jnp.arange(REQ_DEV * TOPK, dtype=jnp.int32)[None, :] // TOPK).astype(jnp.int32)
    slot_token = jnp.full((EXPERTS, DEVICES, CAPACITY), REQUESTS, jnp.int32).at[flat_ids, device_ids, position].set(token_ids)
    padded = jnp.concatenate([hidden, jnp.zeros((1, D), jnp.bfloat16)], axis=0)

    def one_expert(expert_index):
        token_rows = padded[slot_token[expert_index].reshape(DEVICES * CAPACITY)]
        result = expert_rows(token_rows, expert_gate[expert_index], expert_up[expert_index], expert_down[expert_index])
        return result.reshape(DEVICES, CAPACITY, D)
    expert_outputs = lax.map(one_expert, jnp.arange(EXPERTS, dtype=jnp.int32))
    picked = expert_outputs[flat_ids, device_ids, position].reshape(REQUESTS, TOPK, D)
    routed_output = lax.optimization_barrier(jnp.sum(picked * gate_weights[:, :, None], axis=1)).astype(jnp.bfloat16)
    return (context_first, context_second, routed_output)
```

```python
import functools
import math

import jax
import jax.numpy as jnp
from jax import lax
from jax.experimental import pallas as pl
from jax.experimental.pallas import tpu as pltpu
from jax.sharding import PartitionSpec as P

MESH = pl.DeviceIdType.MESH
LATENT = 512
WIDTH = 576
HEADS = 128
CONTEXT = 1024
SLOTS = 8
D = 7168
HALF = D // 2
UNITS = 256
QROWS = 592
X, Y, Z = 0, 1, 2
SCALE = math.log2(math.e) / math.sqrt(192.0)
F32 = jnp.float32
BF16 = jnp.bfloat16

PARTS = (((X, Y, Z), 1280), ((X, Z, Y), 1280), ((Y, Z, X), 512), ((Z, Y, X), 512))
STARTS = (0, 1280, 2560, 3072)
NP = len(PARTS)
MIX = 128


def widths(lanes):
    tiles = lanes // 128
    first = (tiles + 1) // 2 * 128
    return ((0, first), (first, lanes - first))


def kernel(
    lengths, dest, cache, q1, q2, lat1, lat2, hidden, ids, gates, wg, wu, wd,
    out1, out2, routed,
    kt, qa, qb, c1, c2, qg, cg, gw, uw, dw, acc, latt,
    xp0, xp1, xp2, xp3,
    ra0, ra1, ra2, ra3, rb0, rb1, rb2, rb3, rc0, rc1, rc2, rc3,
    sa0, sa1, sa2, sa3, sb0, sb1, sb2, sb3, sc0, sc1, sc2, sc3,
    ag_s, ag_r, rs_s, rs_r, qs, qr, cs, cr, ws, wr, kt_sem, in_sem, o1_sem, o2_sem,
):
    xs = (xp0, xp1, xp2, xp3)
    first_in = ((ra0, ra1, ra2, ra3), (rb0, rb1, rb2, rb3), (rc0, rc1, rc2, rc3))
    last_in = ((sa0, sa1, sa2, sa3), (sb0, sb1, sb2, sb3), (sc0, sc1, sc2, sc3))
    rank = lax.axis_index("req")
    expert = lax.axis_index("exp")
    me = (rank // 2, expert // 4, expert % 4)
    core = rank % 2

    def device(axis, step):
        at = [me[0], me[1], me[2]]
        at[axis] = lax.rem(at[axis] + step, 4)
        return {"req": at[0] * 2 + core, "exp": at[1] * 4 + at[2]}

    def around(axis, step):
        return lax.rem(me[axis] + step, 4)

    sibling = {"req": me[0] * 2 + 1 - core, "exp": expert}

    fetch = [
        pltpu.make_async_copy(q1, qa, in_sem.at[0]),
        pltpu.make_async_copy(q2, qb, in_sem.at[1]),
        pltpu.make_async_copy(wg.at[0], gw.at[0], in_sem.at[2]),
        pltpu.make_async_copy(wu.at[0], uw.at[0], in_sem.at[3]),
        pltpu.make_async_copy(wd.at[0], dw.at[0], in_sem.at[4]),
    ]

    def key_copy(s):
        return pltpu.make_async_copy(cache.at[s], kt.at[s], kt_sem.at[s])

    fetch[1].start()
    fetch[0].start()
    for s in range(SLOTS):
        key_copy(s).start()

    barrier = pltpu.get_barrier_semaphore()
    partners = [sibling] + [device(a, d) for a in range(3) for d in (1, 3)]
    for partner in partners:
        pl.semaphore_signal(barrier, inc=1, device_id=partner, device_id_type=MESH)

    tokens = hidden[...].astype(F32)
    block = jnp.concatenate([tokens[:, :HALF], tokens[:, HALF:]], axis=0).astype(BF16)
    idt = ids[...]
    gatet = gates[...]
    expert_row = lax.broadcasted_iota(jnp.int32, (16, SLOTS), 0)
    mixing = jnp.zeros((16, SLOTS), F32)
    for j in range(4):
        mixing = mixing + jnp.where(expert_row == idt[j : j + 1, :], gatet[j : j + 1, :], 0.0)
    high = mixing.astype(BF16).astype(F32)
    middle = (mixing - high).astype(BF16).astype(F32)
    low = mixing - high - middle
    stacked = jnp.concatenate(
        [high, middle, low, jnp.zeros((MIX - 48, SLOTS), F32)], axis=0
    )
    stacked = jnp.concatenate([stacked, jnp.zeros((MIX, MIX - SLOTS), F32)], axis=1)
    mix_block = stacked.T[:16, :].astype(BF16)
    for p, (_, lanes) in enumerate(PARTS):
        xs[p][me[0], me[1], me[2], :, 0:lanes] = block[:, STARTS[p] : STARTS[p] + lanes]
    xs[0][me[0], me[1], me[2], :, PARTS[0][1] :] = mix_block

    pl.semaphore_wait(barrier, len(partners))

    def region(p, k, at):
        order = PARTS[p][0]
        index = [None, None, None]
        for j, axis in enumerate(order):
            index[axis] = slice(None) if j < k else (at if j == k else me[axis])
        return tuple(index)

    def spread(p, k, m):
        axis = PARTS[p][0][k]
        halves = widths(xs[p].shape[4])
        at, half, step = (
            (me[axis], 0, 1), (me[axis], 1, 3), (me[axis], 1, 1), (me[axis], 0, 3),
            (around(axis, 3), 0, 1), (around(axis, 1), 1, 3),
        )[m]
        start, size = halves[half]
        view = xs[p].at[region(p, k, at) + (slice(None), pl.ds(start, size))]
        return pltpu.make_async_remote_copy(
            src_ref=view, dst_ref=view, send_sem=ag_s.at[p, k, m], recv_sem=ag_r.at[p, k, m],
            device_id=device(axis, step), device_id_type=MESH,
        )

    def spread_start(k):
        for m in range(4):
            for p in range(NP):
                spread(p, k, m).start()

    def spread_forward(k):
        for p in range(NP):
            for m in (0, 1):
                spread(p, k, m).wait_recv()
                spread(p, k, 4 + m).start()

    def spread_wait(k, ms):
        for m in ms:
            for p in range(NP):
                spread(p, k, m).wait_recv()

    def ring(buffer, ss, rs, m):
        if m < 6:
            x, j, step = (
                (me[0], 0, 1), (me[0], 1, 3), (me[0], 1, 1), (me[0], 0, 3),
                (around(X, 3), 0, 1), (around(X, 1), 1, 3),
            )[m]
            view, target = buffer.at[x, core, j], device(X, step)
        else:
            view, target = buffer.at[around(X, (0, 3, 1, 2)[m - 6]), core], sibling
        return pltpu.make_async_remote_copy(
            src_ref=view, dst_ref=view, send_sem=ss.at[m], recv_sem=rs.at[m],
            device_id=target, device_id_type=MESH,
        )

    def ring_start(*args):
        for m in (0, 1, 2, 3, 6):
            ring(*args, m).start()

    def ring_forward(*args):
        for m in (0, 1):
            ring(*args, m).wait_recv()
            ring(*args, 4 + m).start()
        for m in (2, 3):
            ring(*args, m).wait_recv()
        for m in (7, 8):
            ring(*args, m).start()

    def ring_last(*args):
        for m in (4, 5):
            ring(*args, m).wait_recv()
        ring(*args, 9).start()

    def ring_end(*args):
        for m in (6, 7, 8, 9):
            ring(*args, m).wait_recv()
        for m in range(10):
            ring(*args, m).wait_send()

    query_ring = (qg, qs, qr)
    result_ring = (cg, cs, cr)

    spread_start(0)

    own_base = (rank * 16 + expert) * SLOTS
    slot_a = jnp.int32(SLOTS)
    slot_b = jnp.int32(-1)
    for s in range(SLOTS):
        moves = dest[s] != own_base + s
        slot_a = jnp.where(moves, jnp.minimum(slot_a, s), slot_a)
        slot_b = jnp.where(moves, s, slot_b)
    slot_a = jnp.minimum(slot_a, SLOTS - 1)
    slot_b = jnp.maximum(slot_b, 0)
    moving = (slot_a, slot_b)

    fetch[1].wait()
    lane128 = lax.broadcasted_iota(jnp.int32, (16, 128), 1)
    row16 = lax.broadcasted_iota(jnp.int32, (16, 128), 0)
    second_rows = jnp.concatenate(
        [lat2[...].astype(F32), jnp.zeros((SLOTS, 640 - WIDTH), F32)], axis=1
    )
    row8 = lax.broadcasted_iota(jnp.int32, (SLOTS, 640), 0)
    for j in range(2):
        s = moving[j]
        qg[me[0], core, j, 0:WIDTH, :] = qb[s]
        picked = jnp.sum(jnp.where(row8 == s, second_rows, 0.0), axis=0, keepdims=True)
        facts = [s, dest[s] >> 7, dest[s] & 7]
        tail = jnp.zeros((16, 128), F32)
        for i in range(5):
            tail = jnp.where(row16 == i, picked[:, i * 128 : (i + 1) * 128], tail)
        for i, fact in enumerate(facts):
            tail = jnp.where((row16 == 5) & (lane128 == i), fact.astype(F32), tail)
        qg[me[0], core, j, WIDTH:QROWS, :] = tail.astype(BF16)
    ring_start(*query_ring)

    weights = [
        pltpu.make_async_remote_copy(
            src_ref=src.at[0], dst_ref=dst.at[1], send_sem=ws.at[i], recv_sem=wr.at[i],
            device_id=sibling, device_id_type=MESH,
        )
        for i, (src, dst) in enumerate(((wg, gw), (wu, uw), (wd, dw)))
    ]
    for copy in weights:
        copy.start()
    for copy in fetch[2:]:
        copy.start()

    both = jnp.concatenate(
        [lat1[...].astype(F32), lat2[...].astype(F32)], axis=0
    )
    both = jnp.concatenate([both, jnp.zeros((16, 640 - WIDTH), F32)], axis=1)
    both = jnp.concatenate([both, jnp.zeros((112, 640), F32)], axis=0)
    latt[...] = both.T[:WIDTH, :]
    fetch[0].wait()

    lane = lax.broadcasted_iota(jnp.int32, (1, CONTEXT), 1)
    lane_col = lax.broadcasted_iota(jnp.int32, (WIDTH, 128), 1)

    def column(index):
        return jnp.sum(
            jnp.where(lane_col == index, latt[...], 0.0), axis=1, keepdims=True
        ).astype(BF16)

    def weigh(scores, limit):
        scores = jnp.where(lane <= limit, scores, -jnp.inf)
        top = jnp.max(scores, axis=1, keepdims=True)
        weight = jnp.exp2((scores - top) * SCALE)
        return weight.astype(BF16), 1.0 / jnp.sum(weight, axis=1, keepdims=True)

    def out_copy(s):
        return pltpu.make_async_copy(c1.at[s], out1.at[s], o1_sem.at[s])

    def next_phase(k):
        spread_wait(k, (2, 3, 4, 5))
        spread_start(k + 1)

    hooks = {
        1: lambda: spread_forward(0),
        2: lambda: next_phase(0),
        3: lambda: ring_forward(*query_ring),
        4: lambda: spread_forward(1),
        6: lambda: next_phase(1),
    }

    def attend(s, carry):
        for when, hook in hooks.items():
            pl.when(s == when)(hook)
        key_copy(s).wait()
        n = lengths[s]
        keys = jnp.where(
            lane == n, column(s), jnp.where(lane == n + 1, column(SLOTS + s), kt[s])
        )
        kt[s] = keys
        queries = jnp.concatenate([qa[s].T, qb[s].T], axis=0)
        scores = jnp.dot(queries, keys, preferred_element_type=F32)
        prob1, scale1 = weigh(scores[:HEADS], n)
        prob2, scale2 = weigh(scores[HEADS:], n + 1)
        result = lax.dot_general(
            jnp.concatenate([prob1, prob2], axis=0), keys[:LATENT],
            (((1,), (1,)), ((), ())), preferred_element_type=F32,
        )
        c1[s] = (result[:HEADS] * scale1).astype(BF16)
        c2[s] = (result[HEADS:] * scale2).astype(BF16)
        out_copy(s).start()
        return carry

    lax.fori_loop(0, SLOTS, attend, 0)

    ring_last(*query_ring)
    ring_end(*query_ring)

    def fact(r, j, i):
        return qg[r // 2, r % 2, j, WIDTH : WIDTH + 16, :].astype(F32)[5:6, i : i + 1]

    entries = [(r, j) for r in range(8) for j in range(2)]

    def migrant(j, carry):
        s = jnp.where(j == 0, slot_a, slot_b)
        to_rank = (dest[s] >> 7).astype(F32)
        to_slot = (dest[s] & 7).astype(F32)
        query = jnp.zeros((QROWS, HEADS), BF16)
        for r, i in entries:
            hit = (fact(r, i, 0) == to_slot) & (to_rank == r)
            query = query + qg[r // 2, r % 2, i] * jnp.where(hit, 1.0, 0.0).astype(BF16)
        tail = query[WIDTH:QROWS].astype(F32)
        tail = jnp.concatenate([tail, jnp.zeros((112, 128), F32)], axis=0).T
        col = jnp.concatenate(
            [tail[:, i : i + 1] for i in range(4)] + [tail[:64, 4:5]], axis=0
        ).astype(BF16)
        n = lengths[s]
        keys = jnp.where(lane == n + 1, col, kt[s])
        scores = jnp.dot(query[:WIDTH].T, keys, preferred_element_type=F32)
        prob, scale = weigh(scores, n + 1)
        result = lax.dot_general(
            prob, keys[:LATENT], (((1,), (1,)), ((), ())), preferred_element_type=F32
        )
        cg[me[0], core, j] = (result * scale).astype(BF16)
        return carry

    lax.fori_loop(0, 2, migrant, 0)
    ring_start(*result_ring)

    for copy in fetch[2:]:
        copy.wait()
    for copy in weights:
        copy.wait()

    def plane(p, at):
        return region(p, 2, at)

    def project(p, at, fresh):
        lanes = PARTS[p][1]
        total = None
        for h in range(2):
            rows = xs[p][plane(p, at) + (slice(h * 8, h * 8 + 8), slice(0, lanes))]
            rows = rows.astype(F32).reshape(128, lanes).astype(BF16)
            cols = slice(h * HALF + STARTS[p], h * HALF + STARTS[p] + lanes)
            part = [
                jnp.dot(rows, w[i, cols, :], preferred_element_type=F32)
                for w in (gw, uw) for i in range(2)
            ]
            total = part if total is None else [a + b for a, b in zip(total, part)]
        for i, term in enumerate(total):
            where = plane(p, at) + (slice(None), slice(i * UNITS, (i + 1) * UNITS))
            acc[where] = acc[where] + term.reshape(4, 4, 8, UNITS)

    acc[...] = jnp.zeros(acc.shape, F32)

    spread_forward(2)
    for p in range(NP):
        project(p, me[PARTS[p][0][2]], False)
    spread_wait(2, (2, 3))

    for p in range(NP):
        def near(d, carry, p=p):
            project(p, lax.rem(me[PARTS[p][0][2]] + 1 + 2 * d, 4), False)
            return carry
        lax.fori_loop(0, 2, near, 0)
    ring_forward(*result_ring)
    spread_wait(2, (4, 5))
    for p in range(NP):
        project(p, around(PARTS[p][0][2], 2), False)
    for k in range(3):
        for p in range(NP):
            for m in range(6):
                spread(p, k, m).wait_send()

    lane_mix = lax.broadcasted_iota(jnp.int32, (1, MIX), 1)
    chosen = ((lane_mix & 15) == expert) & (lane_mix < 48)

    def activate(x, carry):
        mix = xp0[x, :, :, 0:8, PARTS[0][1] :].astype(F32).reshape(128, MIX)
        weight = jnp.sum(jnp.where(chosen, mix, 0.0), axis=1, keepdims=True)
        gate = acc[x, :, :, :, 0 : 2 * UNITS].reshape(128, 2 * UNITS)
        up = acc[x, :, :, :, 2 * UNITS :].reshape(128, 2 * UNITS)
        inner = gate / (1.0 + jnp.exp(-gate)) * up * weight
        acc[x, :, :, :, 0 : 2 * UNITS] = inner.reshape(4, 4, 8, 2 * UNITS)
        return carry

    lax.fori_loop(0, 4, activate, 0)

    def expand(p, at):
        lanes = PARTS[p][1]
        inner = acc[plane(p, at) + (slice(None), slice(0, 2 * UNITS))]
        inner = inner.reshape(128, 2 * UNITS).astype(BF16)
        halves = []
        for h in range(2):
            cols = slice(h * HALF + STARTS[p], h * HALF + STARTS[p] + lanes)
            value = jnp.dot(inner[:, :UNITS], dw[0, :, cols], preferred_element_type=F32)
            value = value + jnp.dot(inner[:, UNITS:], dw[1, :, cols], preferred_element_type=F32)
            halves.append(value.reshape(4, 4, 8, lanes))
        xs[p][plane(p, at) + (slice(None), slice(0, lanes))] = jnp.concatenate(
            halves, axis=2
        ).astype(BF16)

    def back(p, k, m):
        axis, lanes = PARTS[p][0][k], PARTS[p][1]
        offset, half, step = ((2, 0, 1), (2, 1, 3), (1, 1, 1), (3, 0, 3), (1, 0, 1), (3, 1, 3))[m]
        start, size = widths(lanes)[half]
        view = xs[p].at[region(p, k, around(axis, offset)) + (slice(None), pl.ds(start, size))]
        lead = (slice(None),) * k
        if m < 2:
            first = first_in[2 - k][p]
            into = first.at[(m,) + lead + (slice(None), pl.ds(0, size))]
        else:
            into = last_in[2 - k][p].at[(m % 2,) + lead + (slice(None), pl.ds(start, size))]
        return pltpu.make_async_remote_copy(
            src_ref=view, dst_ref=into, send_sem=rs_s.at[p, k, m], recv_sem=rs_r.at[p, k, m],
            device_id=device(axis, step), device_id_type=MESH,
        )

    def back_join(p, k):
        axis, lanes = PARTS[p][0][k], PARTS[p][1]
        lead = (slice(None),) * k
        for m in (0, 1):
            back(p, k, m).wait_recv()
            start, size = widths(lanes)[m]
            where = region(p, k, around(axis, (1, 3)[m])) + (slice(None), slice(start, start + size))
            came = first_in[2 - k][p][(m,) + lead + (slice(None), slice(0, size))]
            xs[p][where] = (xs[p][where].astype(F32) + came.astype(F32)).astype(BF16)
            back(p, k, 4 + m).start()

    def back_total(p, k):
        axis, lanes = PARTS[p][0][k], PARTS[p][1]
        for m in (2, 3, 4, 5):
            back(p, k, m).wait_recv()
        where = region(p, k, me[axis]) + (slice(None), slice(0, lanes))
        came = last_in[2 - k][p]
        return (
            xs[p][where].astype(F32) + came[0].astype(F32) + came[1].astype(F32)
        ).astype(BF16), where

    for p in range(NP):
        expand(p, around(PARTS[p][0][2], 2))
        back(p, 2, 0).start()
        back(p, 2, 1).start()
    for p in range(NP):
        def near_out(d, carry, p=p):
            expand(p, lax.rem(me[PARTS[p][0][2]] + 1 + 2 * d, 4))
            return carry
        lax.fori_loop(0, 2, near_out, 0)
        back(p, 2, 2).start()
        back(p, 2, 3).start()
    for p in range(NP):
        expand(p, me[PARTS[p][0][2]])
    for p in range(NP):
        back_join(p, 2)
    ring_last(*result_ring)
    for k in (1, 0):
        for p in range(NP):
            total, where = back_total(p, k + 1)
            xs[p][where] = total
            for m in range(4):
                back(p, k, m).start()
        if k == 1:
            ring_end(*result_ring)
            for j in range(2):
                s = moving[j]
                mine = s.astype(F32)
                value = jnp.zeros((HEADS, LATENT), BF16)
                for r, i in entries:
                    hit = (fact(r, i, 1) == rank.astype(F32)) & (fact(r, i, 2) == mine)
                    value = value + cg[r // 2, r % 2, i] * jnp.where(hit, 1.0, 0.0).astype(BF16)
                for t in range(SLOTS):
                    c2[t] = jnp.where(s == t, value, c2[t])
            pltpu.make_async_copy(c2, out2, o2_sem).start()
        for p in range(NP):
            back_join(p, k)
    for p in range(NP):
        total, _ = back_total(p, 0)
        lanes = PARTS[p][1]
        for h in range(2):
            cols = slice(h * HALF + STARTS[p], h * HALF + STARTS[p] + lanes)
            routed[:, cols] = total[h * 8 : h * 8 + 8]
    for k in range(3):
        for p in range(NP):
            for m in range(6):
                back(p, k, m).wait_send()
    for s in range(SLOTS):
        out_copy(s).wait()
    pltpu.make_async_copy(c2, out2, o2_sem).wait()


def shards(
    latent_cache, context_lengths, destination, query_first, latent_first, query_second,
    latent_second, hidden, expert_ids, gate_weights, expert_gate, expert_up, expert_down,
):
    anywhere = pl.BlockSpec(memory_space=pl.ANY)
    vmem = pl.BlockSpec(memory_space=pltpu.VMEM)
    smem = pl.BlockSpec(memory_space=pltpu.SMEM)

    def lead(k):
        return (4,) * k

    xs = [
        pltpu.VMEM((4, 4, 4, 16, lanes + (MIX if p == 0 else 0)), BF16)
        for p, (_, lanes) in enumerate(PARTS)
    ]
    first_in = [
        pltpu.VMEM((2,) + lead(k) + (16, widths(lanes)[0][1]), BF16)
        for k in (2, 1, 0) for _, lanes in PARTS
    ]
    last_in = [
        pltpu.VMEM((2,) + lead(k) + (16, lanes), BF16) for k in (2, 1, 0) for _, lanes in PARTS
    ]
    dma = pltpu.SemaphoreType.DMA
    return pl.pallas_call(
        kernel,
        out_shape=(
            jax.ShapeDtypeStruct((SLOTS, HEADS, LATENT), BF16),
            jax.ShapeDtypeStruct((SLOTS, HEADS, LATENT), BF16),
            jax.ShapeDtypeStruct((SLOTS, D), BF16),
        ),
        in_specs=[smem, smem] + [anywhere] * 3 + [vmem] * 5 + [anywhere] * 3,
        out_specs=(anywhere, anywhere, vmem),
        scratch_shapes=[
            pltpu.VMEM((SLOTS, WIDTH, CONTEXT), BF16),
            pltpu.VMEM((SLOTS, WIDTH, HEADS), BF16),
            pltpu.VMEM((SLOTS, WIDTH, HEADS), BF16),
            pltpu.VMEM((SLOTS, HEADS, LATENT), BF16),
            pltpu.VMEM((SLOTS, HEADS, LATENT), BF16),
            pltpu.VMEM((4, 2, 2, QROWS, HEADS), BF16),
            pltpu.VMEM((4, 2, 2, HEADS, LATENT), BF16),
            pltpu.VMEM((2, D, UNITS), BF16),
            pltpu.VMEM((2, D, UNITS), BF16),
            pltpu.VMEM((2, UNITS, D), BF16),
            pltpu.VMEM((4, 4, 4, 8, 4 * UNITS), F32),
            pltpu.VMEM((WIDTH, 128), F32),
        ]
        + xs + first_in + last_in
        + [
            dma((NP, 3, 6)), dma((NP, 3, 6)), dma((NP, 3, 6)), dma((NP, 3, 6)),
            dma((10,)), dma((10,)), dma((10,)), dma((10,)), dma((3,)), dma((3,)),
            dma((SLOTS,)), dma((5,)), dma((SLOTS,)), dma,
        ],
        compiler_params=pltpu.CompilerParams(
            collective_id=0, has_side_effects=True, vmem_limit_bytes=64 * 1024 * 1024 - 65536
        ),
    )(
        context_lengths, destination,
        jnp.swapaxes(latent_cache, 1, 2), jnp.swapaxes(query_first, 1, 2),
        jnp.swapaxes(query_second, 1, 2), latent_first, latent_second, hidden,
        expert_ids.T, gate_weights.T, expert_gate, expert_up, expert_down,
    )


def solution(mesh):
    rows = P(("req", "exp"), None)
    cubes = P(("req", "exp"), None, None)
    flat = P(("req", "exp"))
    return jax.shard_map(
        shards,
        mesh=mesh,
        in_specs=(
            cubes, flat, flat, cubes, rows, cubes, rows, rows, rows, rows,
            P("exp", None, "req"), P("exp", None, "req"), P("exp", "req", None),
        ),
        out_specs=(cubes, cubes, rows),
        check_vma=False,
    )
```

```python
import functools
import math

import jax
import jax.numpy as jnp
from jax import lax
from jax.experimental import pallas as pl
from jax.experimental.pallas import tpu as pltpu
from jax.sharding import PartitionSpec as P

MESH = pl.DeviceIdType.MESH
LATENT = 512
WIDTH = 576
HEADS = 128
CONTEXT = 1024
SLOTS = 8
D = 7168
HALF = D // 2
UNITS = 256
QROWS = 592
X, Y, Z = 0, 1, 2
SCALE = math.log2(math.e) / math.sqrt(192.0)
F32 = jnp.float32
BF16 = jnp.bfloat16

PARTS = (((X, Y, Z), 1280), ((X, Z, Y), 1280), ((Y, Z, X), 512), ((Z, Y, X), 512))
STARTS = (0, 1280, 2560, 3072)
NP = len(PARTS)
MIX_ORDER = (Y, Z, X)
EARLY = (2, 3)
LATE = (0, 1)


def widths(lanes):
    tiles = lanes // 128
    first = (tiles + 1) // 2 * 128
    return ((0, first), (first, lanes - first))


def dense_axes(p):
    order = PARTS[p][0]
    return tuple(sorted(order[:2] if p in LATE else order[:1]))


def send_phase(p):
    return 2 if p in LATE else 1


def kernel(
    lengths, dest, cache, q1, q2, lat1, lat2, hidden, ids, gates, wg, wu, wd,
    out1, out2, routed,
    kt, qa, qb, c1, c2, qg, cg, gw, uw, dw, acc, latt, xm, perm, inner, wcol,
    xb0, xb1, xb2, xb3, snd0, snd1, snd2, snd3, fin0, fin1, fin2, fin3, ret0, ret1, ret2, ret3,
    sel0, sel1, sel2, sel3, ap1, ap2, ap3,
    fb0, fb1, fb2, fb3, la0, la1, la2, la3, lb0, lb1, lb2, lb3,
    ag_s, ag_r, rs_s, rs_r, to_s, to_r, un_s, un_r, mx_s, mx_r,
    qs, qr, cs, cr, ws, wr, kt_sem, in_sem, o1_sem, o2_sem,
):
    xb = (xb0, xb1, xb2, xb3)
    snd = (snd0, snd1, snd2, snd3)
    fin = (fin0, fin1, fin2, fin3)
    ret = (ret0, ret1, ret2, ret3)
    sels = (sel0, sel1, sel2, sel3)
    partial = (acc, ap1, ap2, ap3)
    first_in = (fb0, fb1, fb2, fb3)
    last_in = (lb0, lb1, lb2, lb3)
    final_in = (la0, la1, la2, la3)
    rank = lax.axis_index("req")
    expert = lax.axis_index("exp")
    me = (rank // 2, expert // 4, expert % 4)
    core = rank % 2

    def device(axis, step):
        at = [me[0], me[1], me[2]]
        at[axis] = lax.rem(at[axis] + step, 4)
        return {"req": at[0] * 2 + core, "exp": at[1] * 4 + at[2]}

    def around(axis, step):
        return lax.rem(me[axis] + step, 4)

    sibling = {"req": me[0] * 2 + 1 - core, "exp": expert}

    fetch = [
        pltpu.make_async_copy(q1, qa, in_sem.at[0]),
        pltpu.make_async_copy(q2, qb, in_sem.at[1]),
        pltpu.make_async_copy(wg.at[0], gw.at[0], in_sem.at[2]),
        pltpu.make_async_copy(wu.at[0], uw.at[0], in_sem.at[3]),
        pltpu.make_async_copy(wd.at[0], dw.at[0], in_sem.at[4]),
    ]

    def key_copy(s):
        return pltpu.make_async_copy(cache.at[s], kt.at[s], kt_sem.at[s])

    fetch[1].start()
    fetch[0].start()
    for s in range(SLOTS):
        key_copy(s).start()

    barrier = pltpu.get_barrier_semaphore()
    partners = [sibling] + [device(a, d) for a in range(3) for d in (1, 2, 3)]
    for partner in partners:
        pl.semaphore_signal(barrier, inc=1, device_id=partner, device_id_type=MESH)

    tokens = hidden[...].astype(F32)
    block = jnp.concatenate([tokens[:, :HALF], tokens[:, HALF:]], axis=0).astype(BF16)
    idt = ids[...]
    gatet = gates[...]
    expert_row = lax.broadcasted_iota(jnp.int32, (128, SLOTS), 0)
    mixing = jnp.zeros((128, SLOTS), F32)
    for j in range(4):
        mixing = mixing + jnp.where(expert_row == idt[j : j + 1, :], gatet[j : j + 1, :], 0.0)
    mixing = jnp.concatenate([mixing, jnp.zeros((128, 128 - SLOTS), F32)], axis=1)
    xm[me[0], me[1], me[2]] = mixing.T[:SLOTS, :]
    for p, (_, lanes) in enumerate(PARTS):
        own = tuple(me[axis] for axis in dense_axes(p))
        xb[p][own] = block[:, STARTS[p] : STARTS[p] + lanes]

    pl.semaphore_wait(barrier, len(partners))

    def area(p, k, at):
        order = PARTS[p][0]
        if k == 2:
            return fin[p], (at, slice(None), slice(None))
        index = {axis: slice(None) for axis in order[:k]}
        index[order[k]] = at
        return xb[p], tuple(index.get(axis, me[axis]) for axis in dense_axes(p))

    def spread(p, k, m):
        axis = PARTS[p][0][k]
        at, half, step = (
            (me[axis], 0, 1), (me[axis], 1, 3), (me[axis], 1, 1), (me[axis], 0, 3),
            (around(axis, 3), 0, 1), (around(axis, 1), 1, 3),
        )[m]
        start, size = widths(PARTS[p][1])[half]
        buffer, index = area(p, k, at)
        view = buffer.at[index + (slice(None), pl.ds(start, size))]
        return pltpu.make_async_remote_copy(
            src_ref=view, dst_ref=view, send_sem=ag_s.at[p, k, m], recv_sem=ag_r.at[p, k, m],
            device_id=device(axis, step), device_id_type=MESH,
        )

    def first_copy(p, step):
        axis = PARTS[p][0][0]
        buffer, index = area(p, 0, me[axis])
        view = buffer.at[index]
        return pltpu.make_async_remote_copy(
            src_ref=view, dst_ref=view, send_sem=ag_s.at[p, 0, step],
            recv_sem=ag_r.at[p, 0, step], device_id=device(axis, step), device_id_type=MESH,
        )

    def spread_start(ps, k):
        for m in range(4):
            for p in ps:
                spread(p, k, m).start()

    def spread_forward(ps, k):
        for p in ps:
            for m in (0, 1):
                spread(p, k, m).wait_recv()
                spread(p, k, 4 + m).start()

    def spread_wait(ps, k, ms):
        for m in ms:
            for p in ps:
                spread(p, k, m).wait_recv()

    def mix_copy(k, step):
        index = {axis: slice(None) for axis in MIX_ORDER[:k]}
        view = xm.at[tuple(index.get(axis, me[axis]) for axis in (X, Y, Z))]
        return pltpu.make_async_remote_copy(
            src_ref=view, dst_ref=view, send_sem=mx_s.at[k, step - 1],
            recv_sem=mx_r.at[k, step - 1], device_id=device(MIX_ORDER[k], step),
            device_id_type=MESH,
        )

    def mix_start(k):
        for step in (2, 1, 3):
            mix_copy(k, step).start()

    def mix_wait(k):
        for step in (1, 2, 3):
            mix_copy(k, step).wait_recv()

    def selector(mix, row_expert, row_block):
        rows, tokens = row_expert.shape[0], mix.shape[0]
        named = lax.broadcasted_iota(jnp.int32, (rows, 128), 1) == row_expert
        weight = lax.dot_general(
            jnp.where(named, 1.0, 0.0).astype(BF16), mix.astype(BF16),
            (((1,), (1,)), ((), ())), preferred_element_type=F32,
        )
        chosen = weight > 0.0
        before = lax.broadcasted_iota(jnp.int32, (tokens, tokens), 0)
        after = lax.broadcasted_iota(jnp.int32, (tokens, tokens), 1)
        earlier = (before // 8 == after // 8) & (before < after)
        position = jnp.dot(
            jnp.where(chosen, 1.0, 0.0).astype(BF16),
            jnp.where(earlier, 1.0, 0.0).astype(BF16), preferred_element_type=F32,
        )
        slot = (lax.broadcasted_iota(jnp.int32, (rows, tokens), 0) % 4).astype(F32)
        token = lax.broadcasted_iota(jnp.int32, (rows, tokens), 1)
        hit = chosen & (position == slot) & (token // 8 == row_block)
        return jnp.where(hit, 1.0, 0.0).astype(BF16)

    def pick_slots(p):
        axis = PARTS[p][0][send_phase(p)]
        dense = dense_axes(p)
        tokens = 8 * 4 ** len(dense)
        where = tuple(slice(None) if a in dense else me[a] for a in (X, Y, Z))
        row = lax.broadcasted_iota(jnp.int32, (2 * tokens, 1), 0)
        target = row // (tokens // 2)
        row_expert = target * 4 + me[Z] if axis == Y else me[Y] * 4 + target
        row_block = (row % (tokens // 2)) // 4
        sels[p][...] = selector(xm[where].reshape(tokens, 128), row_expert, row_block)

    def compact(p, c):
        axis = PARTS[p][0][send_phase(p)]
        dense = len(dense_axes(p))
        tokens = 8 * 4 ** dense
        start, size = chunks(p)[c]
        halves = []
        for h in range(2):
            lead = (slice(None),) * dense
            tok = xb[p][lead + (slice(h * 8, h * 8 + 8), slice(start, start + size))]
            tok = tok.astype(F32).reshape(tokens, size).astype(BF16)
            got = jnp.dot(sels[p][...], tok, preferred_element_type=F32)
            halves.append(got.reshape(4, tokens // 16, 8, size))
        snd[p][:, :, :, start : start + size] = jnp.concatenate(halves, axis=2).astype(BF16)
        for step in (2, 1, 3):
            send(p, c, step).start()
        own = (me[axis],) if p in LATE else (me[X], me[axis])
        lanes = (slice(None), slice(None), slice(start, start + size))
        fin[p][own + lanes] = snd[p][(me[axis],) + lanes]

    def chunks(p):
        return widths(PARTS[p][1]) if p in LATE else ((0, PARTS[p][1]),)

    def send(p, c, step):
        axis = PARTS[p][0][send_phase(p)]
        start, size = chunks(p)[c]
        into = (me[axis],) if p in LATE else (me[X], me[axis])
        rest = (slice(None), slice(None), pl.ds(start, size))
        return pltpu.make_async_remote_copy(
            src_ref=snd[p].at[(around(axis, step),) + rest], dst_ref=fin[p].at[into + rest],
            send_sem=to_s.at[p, c, step - 1], recv_sem=to_r.at[p, c, step - 1],
            device_id=device(axis, step), device_id_type=MESH,
        )

    def send_wait(p, c):
        for step in (1, 3, 2):
            send(p, c, step).wait_recv()

    def ring(buffer, ss, rs, m):
        if m < 6:
            x, j, step = (
                (me[0], 0, 1), (me[0], 1, 3), (me[0], 1, 1), (me[0], 0, 3),
                (around(X, 3), 0, 1), (around(X, 1), 1, 3),
            )[m]
            view, target = buffer.at[x, core, j], device(X, step)
        else:
            view, target = buffer.at[around(X, (0, 3, 1, 2)[m - 6]), core], sibling
        return pltpu.make_async_remote_copy(
            src_ref=view, dst_ref=view, send_sem=ss.at[m], recv_sem=rs.at[m],
            device_id=target, device_id_type=MESH,
        )

    def ring_start(*args):
        for m in (0, 1, 2, 3, 6):
            ring(*args, m).start()

    def ring_forward(*args):
        for m in (0, 1):
            ring(*args, m).wait_recv()
            ring(*args, 4 + m).start()
        for m in (2, 3):
            ring(*args, m).wait_recv()
        for m in (7, 8):
            ring(*args, m).start()

    def ring_last(*args):
        for m in (4, 5):
            ring(*args, m).wait_recv()
        ring(*args, 9).start()

    def ring_end(*args):
        for m in (6, 7, 8, 9):
            ring(*args, m).wait_recv()
        for m in range(10):
            ring(*args, m).wait_send()

    query_ring = (qg, qs, qr)
    result_ring = (cg, cs, cr)

    mix_start(0)
    for step in (2, 1, 3):
        for p in range(NP):
            first_copy(p, step).start()

    own_base = (rank * 16 + expert) * SLOTS
    slot_a = jnp.int32(SLOTS)
    slot_b = jnp.int32(-1)
    for s in range(SLOTS):
        moves = dest[s] != own_base + s
        slot_a = jnp.where(moves, jnp.minimum(slot_a, s), slot_a)
        slot_b = jnp.where(moves, s, slot_b)
    slot_a = jnp.minimum(slot_a, SLOTS - 1)
    slot_b = jnp.maximum(slot_b, 0)
    moving = (slot_a, slot_b)

    fetch[1].wait()
    lane128 = lax.broadcasted_iota(jnp.int32, (16, 128), 1)
    row16 = lax.broadcasted_iota(jnp.int32, (16, 128), 0)
    second_rows = jnp.concatenate(
        [lat2[...].astype(F32), jnp.zeros((SLOTS, 640 - WIDTH), F32)], axis=1
    )
    row8 = lax.broadcasted_iota(jnp.int32, (SLOTS, 640), 0)
    for j in range(2):
        s = moving[j]
        qg[me[0], core, j, 0:WIDTH, :] = qb[s]
        picked = jnp.sum(jnp.where(row8 == s, second_rows, 0.0), axis=0, keepdims=True)
        facts = [s, dest[s] >> 7, dest[s] & 7]
        tail = jnp.zeros((16, 128), F32)
        for i in range(5):
            tail = jnp.where(row16 == i, picked[:, i * 128 : (i + 1) * 128], tail)
        for i, fact in enumerate(facts):
            tail = jnp.where((row16 == 5) & (lane128 == i), fact.astype(F32), tail)
        qg[me[0], core, j, WIDTH:QROWS, :] = tail.astype(BF16)
    weights = [
        pltpu.make_async_remote_copy(
            src_ref=src.at[0], dst_ref=dst.at[1], send_sem=ws.at[i], recv_sem=wr.at[i],
            device_id=sibling, device_id_type=MESH,
        )
        for i, (src, dst) in enumerate(((wg, gw), (wu, uw), (wd, dw)))
    ]
    for copy in weights:
        copy.start()
    for copy in fetch[2:]:
        copy.start()

    both = jnp.concatenate(
        [lat1[...].astype(F32), lat2[...].astype(F32)], axis=0
    )
    both = jnp.concatenate([both, jnp.zeros((16, 640 - WIDTH), F32)], axis=1)
    both = jnp.concatenate([both, jnp.zeros((112, 640), F32)], axis=0)
    latt[...] = both.T[:WIDTH, :]
    fetch[0].wait()

    lane = lax.broadcasted_iota(jnp.int32, (1, CONTEXT), 1)
    lane_col = lax.broadcasted_iota(jnp.int32, (WIDTH, 128), 1)

    def column(index):
        return jnp.sum(
            jnp.where(lane_col == index, latt[...], 0.0), axis=1, keepdims=True
        ).astype(BF16)

    def weigh(scores, limit):
        scores = jnp.where(lane <= limit, scores, -jnp.inf)
        top = jnp.max(scores, axis=1, keepdims=True)
        weight = jnp.exp2((scores - top) * SCALE)
        return weight.astype(BF16), 1.0 / jnp.sum(weight, axis=1, keepdims=True)

    def out_copy(s):
        return pltpu.make_async_copy(c1.at[s], out1.at[s], o1_sem.at[s])

    def hook1():
        for p in range(NP):
            for step in (1, 2, 3):
                first_copy(p, step).wait_recv()
        spread_start(LATE, 1)
        mix_wait(0)
        mix_start(1)
        pick_slots(2)
        compact(2, 0)

    def hook2():
        mix_wait(1)
        mix_start(2)
        pick_slots(3)
        compact(3, 0)

    def hook4():
        for p in EARLY:
            send_wait(p, 0)
        spread_start(EARLY, 2)
        ring_start(*query_ring)

    def hook6():
        mix_wait(2)
        for p in LATE:
            pick_slots(p)

    def hook7():
        spread_wait(LATE, 1, (2, 3, 4, 5))
        for c in range(2):
            for p in LATE:
                compact(p, c)

    hooks = {
        1: hook1,
        2: hook2,
        3: lambda: spread_forward(LATE, 1),
        4: hook4,
        6: hook6,
        7: hook7,
    }

    def attend(s, carry):
        for when, hook in hooks.items():
            pl.when(s == when)(hook)
        key_copy(s).wait()
        n = lengths[s]
        keys = jnp.where(
            lane == n, column(s), jnp.where(lane == n + 1, column(SLOTS + s), kt[s])
        )
        kt[s] = keys
        queries = jnp.concatenate([qa[s].T, qb[s].T], axis=0)
        scores = jnp.dot(queries, keys, preferred_element_type=F32)
        prob1, scale1 = weigh(scores[:HEADS], n)
        prob2, scale2 = weigh(scores[HEADS:], n + 1)
        result = lax.dot_general(
            jnp.concatenate([prob1, prob2], axis=0), keys[:LATENT],
            (((1,), (1,)), ((), ())), preferred_element_type=F32,
        )
        c1[s] = (result[:HEADS] * scale1).astype(BF16)
        c2[s] = (result[HEADS:] * scale2).astype(BF16)
        out_copy(s).start()
        return carry

    lax.fori_loop(0, SLOTS, attend, 0)
    spread_forward(EARLY, 2)

    everyone = xm[...].reshape(512, 128)
    lane_mix = lax.broadcasted_iota(jnp.int32, (16, 128), 1)
    weight_row = lax.dot_general(
        jnp.where(lane_mix == expert, 1.0, 0.0).astype(BF16), everyone.astype(BF16),
        (((1,), (1,)), ((), ())), preferred_element_type=F32,
    )
    chosen_rows = jnp.where(weight_row > 0.0, 1.0, 0.0)
    before = lax.broadcasted_iota(jnp.int32, (512, 512), 0)
    after = lax.broadcasted_iota(jnp.int32, (512, 512), 1)
    earlier = jnp.where((before // 8 == after // 8) & (before < after), 1.0, 0.0).astype(BF16)
    position = jnp.dot(chosen_rows.astype(BF16), earlier, preferred_element_type=F32)[0:1]
    place = jnp.where(chosen_rows[0:1] > 0.0, position, 1000.0)
    token_block = lax.broadcasted_iota(jnp.int32, (1, 512), 1) // 8
    row = lax.broadcasted_iota(jnp.int32, (256, 1), 0)
    row_slot = (row % 4).astype(F32)
    at, hi, lo = row // 64, row // 16 % 4, row // 4 % 4
    row_blocks = (
        hi * 16 + lo * 4 + at, hi * 16 + at * 4 + lo, at * 16 + lo * 4 + hi, at * 16 + hi * 4 + lo
    )

    def slots_of(p):
        hit = (token_block == row_blocks[p]) & (place == row_slot)
        return jnp.where(hit, 1.0, 0.0).astype(BF16)

    common = slots_of(0)
    for p in range(1, NP):
        perm[p - 1] = lax.dot_general(
            common, slots_of(p), (((1,), (1,)), ((), ())), preferred_element_type=F32
        ).astype(BF16)
    rest = jnp.where(lane_mix[0:1] == expert, everyone, 0.0)
    weights_here = jnp.zeros((256, 128), F32)
    for _ in range(3):
        term = rest.astype(BF16)
        weights_here = weights_here + jnp.dot(common, term, preferred_element_type=F32)
        rest = rest - term.astype(F32)
    wcol[...] = jnp.broadcast_to(jnp.sum(weights_here, axis=1, keepdims=True), (256, 128))

    ring_forward(*query_ring)

    for copy in fetch[2:]:
        copy.wait()
    for copy in weights:
        copy.wait()

    def project(p, c):
        start, size = chunks(p)[c]
        lead = (slice(None),) * (len(fin[p].shape) - 2)
        for h in range(2):
            rows = fin[p][lead + (slice(h * 8, h * 8 + 8), slice(start, start + size))]
            rows = rows.astype(F32).reshape(256, size).astype(BF16)
            begin = h * HALF + STARTS[p] + start
            for i in range(4):
                w = (gw, uw)[i // 2]
                term = jnp.dot(rows, w[i % 2, begin : begin + size, :], preferred_element_type=F32)
                cols = slice(i * UNITS, (i + 1) * UNITS)
                if p > 0 and c == 0 and h == 0:
                    partial[p][:, cols] = term
                else:
                    partial[p][:, cols] = partial[p][:, cols] + term

    def merge(p):
        for i in range(4):
            cols = slice(i * UNITS, (i + 1) * UNITS)
            value = partial[p][:, cols]
            high = value.astype(BF16)
            low = (value - high.astype(F32)).astype(BF16)
            moved = jnp.dot(perm[p - 1], high, preferred_element_type=F32)
            moved = moved + jnp.dot(perm[p - 1], low, preferred_element_type=F32)
            acc[:, cols] = acc[:, cols] + moved

    acc[...] = jnp.zeros(acc.shape, F32)

    for p in LATE:
        send_wait(p, 0)
        project(p, 0)
    spread_wait(EARLY, 2, (2, 3, 4, 5))
    for p in EARLY:
        project(p, 0)
        merge(p)
    ring_last(*query_ring)
    for p in (1, 0):
        send_wait(p, 1)
        project(p, 1)
    merge(1)
    for p in range(NP):
        for m in range(6):
            spread(p, 1 if p in LATE else 2, m).wait_send()
        for step in (1, 2, 3):
            first_copy(p, step).wait_send()
        for c in range(len(chunks(p))):
            for step in (1, 2, 3):
                send(p, c, step).wait_send()
    for k in range(3):
        for step in (1, 2, 3):
            mix_copy(k, step).wait_send()

    for i in range(2):
        cols = slice(i * UNITS, (i + 1) * UNITS)
        gate = acc[:, cols]
        up = acc[:, 2 * UNITS + i * UNITS : 2 * UNITS + (i + 1) * UNITS]
        inner[0, :, cols] = (gate / (1.0 + jnp.exp(-gate)) * up * wcol[:, 0:1]).astype(BF16)
    for p in range(1, NP):
        inner[p] = lax.dot_general(
            perm[p - 1], inner[0], (((0,), (0,)), ((), ())), preferred_element_type=F32
        ).astype(BF16)

    def expand(p, c):
        start, size = chunks(p)[c]
        halves = []
        for h in range(2):
            begin = h * HALF + STARTS[p] + start
            cols = slice(begin, begin + size)
            value = jnp.dot(inner[p, :, :UNITS], dw[0, :, cols], preferred_element_type=F32)
            value = value + jnp.dot(
                inner[p, :, UNITS:], dw[1, :, cols], preferred_element_type=F32
            )
            halves.append(value.reshape(fin[p].shape[:-2] + (8, size)))
        lead = (slice(None),) * (len(fin[p].shape) - 1)
        fin[p][lead + (slice(start, start + size),)] = jnp.concatenate(
            halves, axis=len(fin[p].shape) - 2
        ).astype(BF16)

    def unsend(p, c, step):
        axis = PARTS[p][0][send_phase(p)]
        start, size = chunks(p)[c]
        other = around(axis, step)
        rest = (slice(None), slice(None), pl.ds(start, size))
        return pltpu.make_async_remote_copy(
            src_ref=fin[p].at[((other,) if p in LATE else (me[X], other)) + rest],
            dst_ref=ret[p].at[(me[axis],) + rest],
            send_sem=un_s.at[p, c, step - 1], recv_sem=un_r.at[p, c, step - 1],
            device_id=device(axis, step), device_id_type=MESH,
        )

    def unsend_own(p):
        axis = PARTS[p][0][send_phase(p)]
        ret[p][me[axis]] = fin[p][(me[axis],) if p in LATE else (me[X], me[axis])]

    def restore(p, c):
        start, size = chunks(p)[c]
        dense = len(dense_axes(p))
        tokens = 8 * 4 ** dense
        for step in (1, 3, 2):
            unsend(p, c, step).wait_recv()
        halves = []
        for h in range(2):
            rows = ret[p][:, :, h * 8 : h * 8 + 8, start : start + size].astype(F32)
            rows = rows.reshape(2 * tokens, size).astype(BF16)
            value = lax.dot_general(
                sels[p][...], rows, (((0,), (0,)), ((), ())), preferred_element_type=F32
            )
            halves.append(value.reshape((4,) * dense + (8, size)))
        lead = (slice(None),) * (dense + 1)
        xb[p][lead + (slice(start, start + size),)] = jnp.concatenate(
            halves, axis=dense
        ).astype(BF16)

    def back(p, k, m):
        axis, lanes = PARTS[p][0][k], PARTS[p][1]
        offset, half, step = ((2, 0, 1), (2, 1, 3), (1, 1, 1), (3, 0, 3), (1, 0, 1), (3, 1, 3))[m]
        start, size = widths(lanes)[half]
        buffer, index = area(p, k, around(axis, offset))
        view = buffer.at[index + (slice(None), pl.ds(start, size))]
        lead = (slice(None),) * k
        if m < 2:
            into = first_in[p].at[(m,) + lead + (slice(None), pl.ds(0, size))]
        else:
            into = last_in[p].at[(m % 2,) + lead + (slice(None), pl.ds(start, size))]
        return pltpu.make_async_remote_copy(
            src_ref=view, dst_ref=into, send_sem=rs_s.at[p, k, m], recv_sem=rs_r.at[p, k, m],
            device_id=device(axis, step), device_id_type=MESH,
        )

    def back_join(p, k):
        axis, lanes = PARTS[p][0][k], PARTS[p][1]
        lead = (slice(None),) * k
        for m in (0, 1):
            back(p, k, m).wait_recv()
            start, size = widths(lanes)[m]
            buffer, index = area(p, k, around(axis, (1, 3)[m]))
            where = index + (slice(None), slice(start, start + size))
            came = first_in[p][(m,) + lead + (slice(None), slice(0, size))]
            buffer[where] = (buffer[where].astype(F32) + came.astype(F32)).astype(BF16)
            back(p, k, 4 + m).start()

    def back_total(p, k):
        axis = PARTS[p][0][k]
        for m in (2, 3, 4, 5):
            back(p, k, m).wait_recv()
        buffer, index = area(p, k, me[axis])
        came = last_in[p]
        total = buffer[index].astype(F32) + came[0].astype(F32) + came[1].astype(F32)
        return total.astype(BF16), buffer, index

    def back_start(p, k):
        for m in range(4):
            back(p, k, m).start()

    def last_copy(p, step):
        axis = PARTS[p][0][0]
        buffer, index = area(p, 0, around(axis, step))
        return pltpu.make_async_remote_copy(
            src_ref=buffer.at[index], dst_ref=final_in[p].at[step - 1],
            send_sem=rs_s.at[p, 0, step], recv_sem=rs_r.at[p, 0, step],
            device_id=device(axis, step), device_id_type=MESH,
        )

    def last_start(p):
        for step in (2, 1, 3):
            last_copy(p, step).start()

    def last_total(p):
        buffer, index = area(p, 0, me[PARTS[p][0][0]])
        total = buffer[index].astype(F32)
        for step in (1, 3, 2):
            last_copy(p, step).wait_recv()
            total = total + final_in[p][step - 1].astype(F32)
        return total.astype(BF16)

    def expand_late(c):
        for p in LATE:
            expand(p, c)
            for step in (2, 1, 3):
                unsend(p, c, step).start()

    expand_late(0)
    for p in EARLY:
        expand(p, 0)
        back_start(p, 2)
    expand_late(1)
    for p in LATE:
        unsend_own(p)
    ring_end(*query_ring)

    def fact(r, j, i):
        return qg[r // 2, r % 2, j, WIDTH : WIDTH + 16, :].astype(F32)[5:6, i : i + 1]

    entries = [(r, j) for r in range(8) for j in range(2)]

    def migrant(j, carry):
        s = jnp.where(j == 0, slot_a, slot_b)
        to_rank = (dest[s] >> 7).astype(F32)
        to_slot = (dest[s] & 7).astype(F32)
        query = jnp.zeros((QROWS, HEADS), BF16)
        for r, i in entries:
            hit = (fact(r, i, 0) == to_slot) & (to_rank == r)
            query = query + qg[r // 2, r % 2, i] * jnp.where(hit, 1.0, 0.0).astype(BF16)
        tail = query[WIDTH:QROWS].astype(F32)
        tail = jnp.concatenate([tail, jnp.zeros((112, 128), F32)], axis=0).T
        col = jnp.concatenate(
            [tail[:, i : i + 1] for i in range(4)] + [tail[:64, 4:5]], axis=0
        ).astype(BF16)
        n = lengths[s]
        keys = jnp.where(lane == n + 1, col, kt[s])
        scores = jnp.dot(query[:WIDTH].T, keys, preferred_element_type=F32)
        prob, scale = weigh(scores, n + 1)
        result = lax.dot_general(
            prob, keys[:LATENT], (((1,), (1,)), ((), ())), preferred_element_type=F32
        )
        cg[me[0], core, j] = (result * scale).astype(BF16)
        return carry

    lax.fori_loop(0, 2, migrant, 0)
    ring_start(*result_ring)

    for p in EARLY:
        back_join(p, 2)
    for p in LATE:
        restore(p, 0)
        back(p, 1, 0).start()
        back(p, 1, 3).start()
    ring_forward(*result_ring)
    for p in EARLY:
        total, buffer, index = back_total(p, 2)
        buffer[index] = total
        for step in (2, 1, 3):
            unsend(p, 0, step).start()
        unsend_own(p)
    for p in LATE:
        restore(p, 1)
        back(p, 1, 1).start()
        back(p, 1, 2).start()
    ring_last(*result_ring)
    for p in LATE:
        back_join(p, 1)
    for p in EARLY:
        restore(p, 0)
        last_start(p)
    for p in LATE:
        total, buffer, index = back_total(p, 1)
        buffer[index] = total
        last_start(p)
    ring_end(*result_ring)
    for j in range(2):
        s = moving[j]
        mine = s.astype(F32)
        value = jnp.zeros((HEADS, LATENT), BF16)
        for r, i in entries:
            hit = (fact(r, i, 1) == rank.astype(F32)) & (fact(r, i, 2) == mine)
            value = value + cg[r // 2, r % 2, i] * jnp.where(hit, 1.0, 0.0).astype(BF16)
        for t in range(SLOTS):
            c2[t] = jnp.where(s == t, value, c2[t])
    pltpu.make_async_copy(c2, out2, o2_sem).start()
    for p in EARLY + LATE:
        total = last_total(p)
        lanes = PARTS[p][1]
        for h in range(2):
            cols = slice(h * HALF + STARTS[p], h * HALF + STARTS[p] + lanes)
            routed[:, cols] = total[h * 8 : h * 8 + 8]
    for p in range(NP):
        for m in range(6):
            back(p, 1 if p in LATE else 2, m).wait_send()
        for step in (1, 2, 3):
            last_copy(p, step).wait_send()
        for c in range(len(chunks(p))):
            for step in (1, 2, 3):
                unsend(p, c, step).wait_send()
    for s in range(SLOTS):
        out_copy(s).wait()
    pltpu.make_async_copy(c2, out2, o2_sem).wait()


def finish(first, second, tokens, out1, out2, routed, held, sem_in, sem_out):
    pairs = [(i, s) for i in range(2) for s in range(0, SLOTS, 2)]
    sources, targets = (first, second), (out1, out2)

    def inward(i, s):
        return pltpu.make_async_copy(
            sources[i].at[pl.ds(s, 2)], held.at[i, pl.ds(s, 2)], sem_in.at[i, s]
        )

    def outward(i, s):
        return pltpu.make_async_copy(
            held.at[i, pl.ds(s, 2)], targets[i].at[pl.ds(s, 2)], sem_out.at[i, s]
        )

    for pair in pairs:
        inward(*pair).start()
    routed[...] = tokens[...]
    for pair in pairs:
        inward(*pair).wait()
        outward(*pair).start()
    for pair in pairs:
        outward(*pair).wait()


def shards(
    latent_cache, context_lengths, destination, query_first, latent_first, query_second,
    latent_second, hidden, expert_ids, gate_weights, expert_gate, expert_up, expert_down,
):
    anywhere = pl.BlockSpec(memory_space=pl.ANY)
    vmem = pl.BlockSpec(memory_space=pltpu.VMEM)
    smem = pl.BlockSpec(memory_space=pltpu.SMEM)

    def each(shape):
        return [pltpu.VMEM(shape(p, PARTS[p][1]), BF16) for p in range(NP)]

    def groups(p):
        return 8 if p in LATE else 2

    def ring_lead(p):
        return (4,) if p in LATE else (4, 2)

    buffers = (
        each(lambda p, lanes: (4,) * len(dense_axes(p)) + (16, lanes))
        + each(lambda p, lanes: (4, groups(p), 16, lanes))
        + each(lambda p, lanes: (4, 8, 16, lanes) if p in LATE else (4, 4, 2, 16, lanes))
        + each(lambda p, lanes: (4, groups(p), 16, lanes))
        + each(lambda p, lanes: (32 * groups(p), 16 * groups(p)))
        + [pltpu.VMEM((256, 4 * UNITS), F32) for _ in range(NP - 1)]
        + each(lambda p, lanes: (2,) + ring_lead(p) + (16, widths(lanes)[0][1]))
        + each(lambda p, lanes: (3, 16, lanes))
        + each(lambda p, lanes: (2,) + ring_lead(p) + (16, lanes))
    )
    dma = pltpu.SemaphoreType.DMA
    shapes = (
        jax.ShapeDtypeStruct((SLOTS, HEADS, LATENT), BF16),
        jax.ShapeDtypeStruct((SLOTS, HEADS, LATENT), BF16),
        jax.ShapeDtypeStruct((SLOTS, D), BF16),
    )
    results = pl.pallas_call(
        kernel,
        out_shape=shapes,
        in_specs=[smem, smem] + [anywhere] * 3 + [vmem] * 5 + [anywhere] * 3,
        out_specs=(anywhere, anywhere, vmem),
        scratch_shapes=[
            pltpu.VMEM((SLOTS, WIDTH, CONTEXT), BF16),
            pltpu.VMEM((SLOTS, WIDTH, HEADS), BF16),
            pltpu.VMEM((SLOTS, WIDTH, HEADS), BF16),
            pltpu.VMEM((SLOTS, HEADS, LATENT), BF16),
            pltpu.VMEM((SLOTS, HEADS, LATENT), BF16),
            pltpu.VMEM((4, 2, 2, QROWS, HEADS), BF16),
            pltpu.VMEM((4, 2, 2, HEADS, LATENT), BF16),
            pltpu.VMEM((2, D, UNITS), BF16),
            pltpu.VMEM((2, D, UNITS), BF16),
            pltpu.VMEM((2, UNITS, D), BF16),
            pltpu.VMEM((256, 4 * UNITS), F32),
            pltpu.VMEM((WIDTH, 128), F32),
            pltpu.VMEM((4, 4, 4, SLOTS, 128), F32),
            pltpu.VMEM((3, 256, 256), BF16),
            pltpu.VMEM((NP, 256, 2 * UNITS), BF16),
            pltpu.VMEM((256, 128), F32),
        ]
        + buffers
        + [
            dma((NP, 3, 6)), dma((NP, 3, 6)), dma((NP, 3, 6)), dma((NP, 3, 6)),
            dma((NP, 2, 3)), dma((NP, 2, 3)), dma((NP, 2, 3)), dma((NP, 2, 3)),
            dma((3, 3)), dma((3, 3)),
            dma((10,)), dma((10,)), dma((10,)), dma((10,)), dma((3,)), dma((3,)),
            dma((SLOTS,)), dma((5,)), dma((SLOTS,)), dma,
        ],
        compiler_params=pltpu.CompilerParams(
            collective_id=0, has_side_effects=True, vmem_limit_bytes=64 * 1024 * 1024 - 65536
        ),
    )(
        context_lengths, destination,
        jnp.swapaxes(latent_cache, 1, 2), jnp.swapaxes(query_first, 1, 2),
        jnp.swapaxes(query_second, 1, 2), latent_first, latent_second, hidden,
        expert_ids.T, gate_weights.T, expert_gate, expert_up, expert_down,
    )
    return pl.pallas_call(
        finish,
        out_shape=shapes,
        in_specs=[anywhere, anywhere, vmem],
        out_specs=(anywhere, anywhere, vmem),
        scratch_shapes=[
            pltpu.VMEM((2, SLOTS, HEADS, LATENT), BF16), dma((2, SLOTS)), dma((2, SLOTS)),
        ],
    )(*results)


def solution(mesh):
    rows = P(("req", "exp"), None)
    cubes = P(("req", "exp"), None, None)
    flat = P(("req", "exp"))
    return jax.shard_map(
        shards,
        mesh=mesh,
        in_specs=(
            cubes, flat, flat, cubes, rows, cubes, rows, rows, rows, rows,
            P("exp", None, "req"), P("exp", None, "req"), P("exp", "req", None),
        ),
        out_specs=(cubes, cubes, rows),
        check_vma=False,
    )
```

```python
import functools
import math

import jax
import jax.numpy as jnp
from jax import lax
from jax.experimental import pallas as pl
from jax.experimental.pallas import tpu as pltpu
from jax.sharding import PartitionSpec as P

MESH = pl.DeviceIdType.MESH
LATENT = 512
WIDTH = 576
HEADS = 128
CONTEXT = 1024
SLOTS = 8
D = 7168
HALF = D // 2
UNITS = 256
QROWS = 592
X, Y, Z = 0, 1, 2
SCALE = math.log2(math.e) / math.sqrt(192.0)
F32 = jnp.float32
BF16 = jnp.bfloat16

PARTS = (((X, Y, Z), 1408), ((X, Z, Y), 1408), ((Y, Z, X), 384), ((Z, Y, X), 384))
STARTS = (0, 1408, 2816, 3200)
NP = len(PARTS)
MIX_ORDER = (Y, Z, X)
EARLY = (2, 3)
LATE = (0, 1)


def widths(lanes):
    tiles = lanes // 128
    first = (tiles + 1) // 2 * 128
    return ((0, first), (first, lanes - first))


def dense_axes(p):
    order = PARTS[p][0]
    return tuple(sorted(order[:2] if p in LATE else order[:1]))


def send_phase(p):
    return 2 if p in LATE else 1


def kernel(
    lengths, dest, cache, q1, q2, lat1, lat2, hidden, ids, gates, wg, wu, wd,
    out1, out2, routed,
    kt, qa, qb, c1, c2, qg, cg, gw, uw, dw, acc, latt, xm, perm, inner, wcol,
    xb0, xb1, xb2, xb3, snd0, snd1, snd2, snd3, fin0, fin1, fin2, fin3, ret0, ret1, ret2, ret3,
    sel0, sel1, sel2, sel3,
    fb0, fb1, fb2, fb3, la0, la1, la2, la3, lb0, lb1, lb2, lb3,
    ag_s, ag_r, rs_s, rs_r, to_s, to_r, un_s, un_r, mx_s, mx_r,
    qs, qr, cs, cr, ws, wr, kt_sem, in_sem, o1_sem, o2_sem,
):
    xb = (xb0, xb1, xb2, xb3)
    snd = (snd0, snd1, snd2, snd3)
    fin = (fin0, fin1, fin2, fin3)
    ret = (ret0, ret1, ret2, ret3)
    sels = (sel0, sel1, sel2, sel3)
    first_in = (fb0, fb1, fb2, fb3)
    last_in = (lb0, lb1, lb2, lb3)
    final_in = (la0, la1, la2, la3)
    rank = lax.axis_index("req")
    expert = lax.axis_index("exp")
    me = (rank // 2, expert // 4, expert % 4)
    core = rank % 2

    def device(axis, step):
        at = [me[0], me[1], me[2]]
        at[axis] = lax.rem(at[axis] + step, 4)
        return {"req": at[0] * 2 + core, "exp": at[1] * 4 + at[2]}

    def around(axis, step):
        return lax.rem(me[axis] + step, 4)

    sibling = {"req": me[0] * 2 + 1 - core, "exp": expert}

    fetch = [
        pltpu.make_async_copy(q1, qa, in_sem.at[0]),
        pltpu.make_async_copy(q2, qb, in_sem.at[1]),
        pltpu.make_async_copy(wg.at[0], gw.at[0], in_sem.at[2]),
        pltpu.make_async_copy(wu.at[0], uw.at[0], in_sem.at[3]),
        pltpu.make_async_copy(wd.at[0], dw.at[0], in_sem.at[4]),
    ]

    def key_copy(s):
        return pltpu.make_async_copy(cache.at[s], kt.at[s], kt_sem.at[s])

    fetch[1].start()
    fetch[0].start()
    for s in range(SLOTS):
        key_copy(s).start()

    barrier = pltpu.get_barrier_semaphore()
    partners = [sibling] + [device(a, d) for a in range(3) for d in (1, 2, 3)]
    for partner in partners:
        pl.semaphore_signal(barrier, inc=1, device_id=partner, device_id_type=MESH)

    tokens = hidden[...].astype(F32)
    block = jnp.concatenate([tokens[:, :HALF], tokens[:, HALF:]], axis=0).astype(BF16)
    idt = ids[...]
    gatet = gates[...]
    expert_row = lax.broadcasted_iota(jnp.int32, (128, SLOTS), 0)
    mixing = jnp.zeros((128, SLOTS), F32)
    for j in range(4):
        mixing = mixing + jnp.where(expert_row == idt[j : j + 1, :], gatet[j : j + 1, :], 0.0)
    mixing = jnp.concatenate([mixing, jnp.zeros((128, 128 - SLOTS), F32)], axis=1)
    xm[me[0], me[1], me[2]] = mixing.T[:SLOTS, :]
    for p, (_, lanes) in enumerate(PARTS):
        own = tuple(me[axis] for axis in dense_axes(p))
        xb[p][own] = block[:, STARTS[p] : STARTS[p] + lanes]

    pl.semaphore_wait(barrier, len(partners))

    def area(p, k, at):
        order = PARTS[p][0]
        if k == 2:
            return fin[p], (at, slice(None), slice(None))
        index = {axis: slice(None) for axis in order[:k]}
        index[order[k]] = at
        return xb[p], tuple(index.get(axis, me[axis]) for axis in dense_axes(p))

    def spread(p, k, m):
        axis = PARTS[p][0][k]
        at, half, step = (
            (me[axis], 0, 1), (me[axis], 1, 3), (me[axis], 1, 1), (me[axis], 0, 3),
            (around(axis, 3), 0, 1), (around(axis, 1), 1, 3),
        )[m]
        start, size = widths(PARTS[p][1])[half]
        buffer, index = area(p, k, at)
        view = buffer.at[index + (slice(None), pl.ds(start, size))]
        return pltpu.make_async_remote_copy(
            src_ref=view, dst_ref=view, send_sem=ag_s.at[p, k, m], recv_sem=ag_r.at[p, k, m],
            device_id=device(axis, step), device_id_type=MESH,
        )

    def spread_start(ps, k):
        for m in range(4):
            for p in ps:
                spread(p, k, m).start()

    def spread_forward(ps, k):
        for p in ps:
            for m in (0, 1):
                spread(p, k, m).wait_recv()
                spread(p, k, 4 + m).start()

    def spread_wait(ps, k, ms):
        for m in ms:
            for p in ps:
                spread(p, k, m).wait_recv()

    def mix_copy(k, step):
        index = {axis: slice(None) for axis in MIX_ORDER[:k]}
        view = xm.at[tuple(index.get(axis, me[axis]) for axis in (X, Y, Z))]
        return pltpu.make_async_remote_copy(
            src_ref=view, dst_ref=view, send_sem=mx_s.at[k, step - 1],
            recv_sem=mx_r.at[k, step - 1], device_id=device(MIX_ORDER[k], step),
            device_id_type=MESH,
        )

    def mix_start(k):
        for step in (2, 1, 3):
            mix_copy(k, step).start()

    def mix_wait(k):
        for step in (1, 2, 3):
            mix_copy(k, step).wait_recv()

    def selector(mix, row_expert, row_block):
        rows, tokens = row_expert.shape[0], mix.shape[0]
        named = lax.broadcasted_iota(jnp.int32, (rows, 128), 1) == row_expert
        weight = lax.dot_general(
            jnp.where(named, 1.0, 0.0).astype(BF16), mix.astype(BF16),
            (((1,), (1,)), ((), ())), preferred_element_type=F32,
        )
        chosen = weight > 0.0
        before = lax.broadcasted_iota(jnp.int32, (tokens, tokens), 0)
        after = lax.broadcasted_iota(jnp.int32, (tokens, tokens), 1)
        earlier = (before // 8 == after // 8) & (before < after)
        position = jnp.dot(
            jnp.where(chosen, 1.0, 0.0).astype(BF16),
            jnp.where(earlier, 1.0, 0.0).astype(BF16), preferred_element_type=F32,
        )
        slot = (lax.broadcasted_iota(jnp.int32, (rows, tokens), 0) % 4).astype(F32)
        token = lax.broadcasted_iota(jnp.int32, (rows, tokens), 1)
        hit = chosen & (position == slot) & (token // 8 == row_block)
        return jnp.where(hit, 1.0, 0.0).astype(BF16)

    def pick_slots(p):
        axis = PARTS[p][0][send_phase(p)]
        dense = dense_axes(p)
        tokens = 8 * 4 ** len(dense)
        where = tuple(slice(None) if a in dense else me[a] for a in (X, Y, Z))
        row = lax.broadcasted_iota(jnp.int32, (2 * tokens, 1), 0)
        target = row // (tokens // 2)
        row_expert = target * 4 + me[Z] if axis == Y else me[Y] * 4 + target
        row_block = (row % (tokens // 2)) // 4
        sels[p][...] = selector(xm[where].reshape(tokens, 128), row_expert, row_block)

    def compact(p, c):
        axis = PARTS[p][0][send_phase(p)]
        dense = len(dense_axes(p))
        tokens = 8 * 4 ** dense
        start, size = chunks(p)[c]
        halves = []
        for h in range(2):
            lead = (slice(None),) * dense
            tok = xb[p][lead + (slice(h * 8, h * 8 + 8), slice(start, start + size))]
            tok = tok.astype(F32).reshape(tokens, size).astype(BF16)
            got = jnp.dot(sels[p][...], tok, preferred_element_type=F32)
            halves.append(got.reshape(4, tokens // 16, 8, size))
        snd[p][:, :, :, start : start + size] = jnp.concatenate(halves, axis=2).astype(BF16)
        for step in (2, 1, 3):
            send(p, c, step).start()
        own = (me[axis],) if p in LATE else (me[X], me[axis])
        lanes = (slice(None), slice(None), slice(start, start + size))
        fin[p][own + lanes] = snd[p][(me[axis],) + lanes]

    def chunks(p):
        return widths(PARTS[p][1]) if p in LATE else ((0, PARTS[p][1]),)

    def send(p, c, step):
        axis = PARTS[p][0][send_phase(p)]
        start, size = chunks(p)[c]
        into = (me[axis],) if p in LATE else (me[X], me[axis])
        rest = (slice(None), slice(None), pl.ds(start, size))
        return pltpu.make_async_remote_copy(
            src_ref=snd[p].at[(around(axis, step),) + rest], dst_ref=fin[p].at[into + rest],
            send_sem=to_s.at[p, c, step - 1], recv_sem=to_r.at[p, c, step - 1],
            device_id=device(axis, step), device_id_type=MESH,
        )

    def send_wait(p, c):
        for step in (1, 3, 2):
            send(p, c, step).wait_recv()

    def ring(buffer, ss, rs, m):
        if m < 6:
            x, j, step = (
                (me[0], 0, 1), (me[0], 1, 3), (me[0], 1, 1), (me[0], 0, 3),
                (around(X, 3), 0, 1), (around(X, 1), 1, 3),
            )[m]
            view, target = buffer.at[x, core, j], device(X, step)
        else:
            view, target = buffer.at[around(X, (0, 3, 1, 2)[m - 6]), core], sibling
        return pltpu.make_async_remote_copy(
            src_ref=view, dst_ref=view, send_sem=ss.at[m], recv_sem=rs.at[m],
            device_id=target, device_id_type=MESH,
        )

    def ring_start(*args):
        for m in (0, 1, 2, 3, 6):
            ring(*args, m).start()

    def ring_forward(*args):
        for m in (0, 1):
            ring(*args, m).wait_recv()
            ring(*args, 4 + m).start()
        for m in (2, 3):
            ring(*args, m).wait_recv()
        for m in (7, 8):
            ring(*args, m).start()

    def ring_last(*args):
        for m in (4, 5):
            ring(*args, m).wait_recv()
        ring(*args, 9).start()

    def ring_end(*args):
        for m in (6, 7, 8, 9):
            ring(*args, m).wait_recv()
        for m in range(10):
            ring(*args, m).wait_send()

    query_ring = (qg, qs, qr)
    result_ring = (cg, cs, cr)

    mix_start(0)
    spread_start(range(NP), 0)

    weights = [
        pltpu.make_async_remote_copy(
            src_ref=src.at[0], dst_ref=dst.at[1], send_sem=ws.at[i], recv_sem=wr.at[i],
            device_id=sibling, device_id_type=MESH,
        )
        for i, (src, dst) in enumerate(((wg, gw), (wu, uw), (wd, dw)))
    ]
    for copy in weights:
        copy.start()
    for copy in fetch[2:]:
        copy.start()

    own_base = (rank * 16 + expert) * SLOTS
    slot_a = jnp.int32(SLOTS)
    slot_b = jnp.int32(-1)
    for s in range(SLOTS):
        moves = dest[s] != own_base + s
        slot_a = jnp.where(moves, jnp.minimum(slot_a, s), slot_a)
        slot_b = jnp.where(moves, s, slot_b)
    slot_a = jnp.minimum(slot_a, SLOTS - 1)
    slot_b = jnp.maximum(slot_b, 0)
    moving = (slot_a, slot_b)

    fetch[1].wait()
    lane128 = lax.broadcasted_iota(jnp.int32, (16, 128), 1)
    row16 = lax.broadcasted_iota(jnp.int32, (16, 128), 0)
    second_rows = jnp.concatenate(
        [lat2[...].astype(F32), jnp.zeros((SLOTS, 640 - WIDTH), F32)], axis=1
    )
    row8 = lax.broadcasted_iota(jnp.int32, (SLOTS, 640), 0)
    for j in range(2):
        s = moving[j]
        qg[me[0], core, j, 0:WIDTH, :] = qb[s]
        picked = jnp.sum(jnp.where(row8 == s, second_rows, 0.0), axis=0, keepdims=True)
        facts = [s, dest[s] >> 7, dest[s] & 7]
        tail = jnp.zeros((16, 128), F32)
        for i in range(5):
            tail = jnp.where(row16 == i, picked[:, i * 128 : (i + 1) * 128], tail)
        for i, fact in enumerate(facts):
            tail = jnp.where((row16 == 5) & (lane128 == i), fact.astype(F32), tail)
        qg[me[0], core, j, WIDTH:QROWS, :] = tail.astype(BF16)
    both = jnp.concatenate(
        [lat1[...].astype(F32), lat2[...].astype(F32)], axis=0
    )
    both = jnp.concatenate([both, jnp.zeros((16, 640 - WIDTH), F32)], axis=1)
    both = jnp.concatenate([both, jnp.zeros((112, 640), F32)], axis=0)
    latt[...] = both.T[:WIDTH, :]
    fetch[0].wait()

    lane = lax.broadcasted_iota(jnp.int32, (1, CONTEXT), 1)
    lane_col = lax.broadcasted_iota(jnp.int32, (WIDTH, 128), 1)

    def column(index):
        return jnp.sum(
            jnp.where(lane_col == index, latt[...], 0.0), axis=1, keepdims=True
        ).astype(BF16)

    def weigh(scores, limit):
        scores = jnp.where(lane <= limit, scores, -jnp.inf)
        top = jnp.max(scores, axis=1, keepdims=True)
        weight = jnp.exp2((scores - top) * SCALE)
        return weight.astype(BF16), 1.0 / jnp.sum(weight, axis=1, keepdims=True)

    def out_copy(s):
        return pltpu.make_async_copy(c1.at[s], out1.at[s], o1_sem.at[s])

    def hook1():
        spread_forward(range(NP), 0)
        spread_wait(range(NP), 0, (2, 3, 4, 5))
        spread_start(LATE, 1)
        mix_wait(0)
        mix_start(1)
        pick_slots(2)
        compact(2, 0)

    def hook2():
        mix_wait(1)
        mix_start(2)
        pick_slots(3)
        compact(3, 0)

    def hook4():
        for p in EARLY:
            send_wait(p, 0)
        spread_start(EARLY, 2)
        ring_start(*query_ring)

    def hook6():
        mix_wait(2)
        for p in LATE:
            pick_slots(p)

    def hook7():
        hook6()
        spread_wait(LATE, 1, (2, 3, 4, 5))
        for c in range(2):
            for p in LATE:
                compact(p, c)

    hooks = {
        1: hook1,
        2: hook2,
        3: lambda: spread_forward(LATE, 1),
        4: hook4,
        5: hook7,
    }

    def attend(s, carry):
        for when, hook in hooks.items():
            pl.when(s == when)(hook)
        key_copy(s).wait()
        n = lengths[s]
        keys = jnp.where(
            lane == n, column(s), jnp.where(lane == n + 1, column(SLOTS + s), kt[s])
        )
        kt[s] = keys
        queries = jnp.concatenate([qa[s].T, qb[s].T], axis=0)
        scores = jnp.dot(queries, keys, preferred_element_type=F32)
        prob1, scale1 = weigh(scores[:HEADS], n)
        prob2, scale2 = weigh(scores[HEADS:], n + 1)
        result = lax.dot_general(
            jnp.concatenate([prob1, prob2], axis=0), keys[:LATENT],
            (((1,), (1,)), ((), ())), preferred_element_type=F32,
        )
        c1[s] = (result[:HEADS] * scale1).astype(BF16)
        c2[s] = (result[HEADS:] * scale2).astype(BF16)
        out_copy(s).start()
        return carry

    lax.fori_loop(0, SLOTS, attend, 0)
    spread_forward(EARLY, 2)

    everyone = xm[...].reshape(512, 128)
    lane_mix = lax.broadcasted_iota(jnp.int32, (16, 128), 1)
    weight_row = lax.dot_general(
        jnp.where(lane_mix == expert, 1.0, 0.0).astype(BF16), everyone.astype(BF16),
        (((1,), (1,)), ((), ())), preferred_element_type=F32,
    )
    chosen_rows = jnp.where(weight_row > 0.0, 1.0, 0.0)
    before = lax.broadcasted_iota(jnp.int32, (512, 512), 0)
    after = lax.broadcasted_iota(jnp.int32, (512, 512), 1)
    earlier = jnp.where((before // 8 == after // 8) & (before < after), 1.0, 0.0).astype(BF16)
    position = jnp.dot(chosen_rows.astype(BF16), earlier, preferred_element_type=F32)[0:1]
    place = jnp.where(chosen_rows[0:1] > 0.0, position, 1000.0)
    token_block = lax.broadcasted_iota(jnp.int32, (1, 512), 1) // 8
    row = lax.broadcasted_iota(jnp.int32, (256, 1), 0)
    row_slot = (row % 4).astype(F32)
    at, hi, lo = row // 64, row // 16 % 4, row // 4 % 4
    row_blocks = (
        hi * 16 + lo * 4 + at, hi * 16 + at * 4 + lo, at * 16 + lo * 4 + hi, at * 16 + hi * 4 + lo
    )

    def slots_of(p):
        hit = (token_block == row_blocks[p]) & (place == row_slot)
        return jnp.where(hit, 1.0, 0.0).astype(BF16)

    common = slots_of(0)
    for p in range(1, NP):
        perm[p - 1] = lax.dot_general(
            common, slots_of(p), (((1,), (1,)), ((), ())), preferred_element_type=F32
        ).astype(BF16)
    rest = jnp.where(lane_mix[0:1] == expert, everyone, 0.0)
    weights_here = jnp.zeros((256, 128), F32)
    for _ in range(3):
        term = rest.astype(BF16)
        weights_here = weights_here + jnp.dot(common, term, preferred_element_type=F32)
        rest = rest - term.astype(F32)
    wcol[...] = jnp.broadcast_to(jnp.sum(weights_here, axis=1, keepdims=True), (256, 128))

    ring_forward(*query_ring)

    for copy in fetch[2:4] + weights[:2]:
        copy.wait()

    def project(p, c):
        start, size = chunks(p)[c]
        lead = (slice(None),) * (len(fin[p].shape) - 2)
        for h in range(2):
            rows = fin[p][lead + (slice(h * 8, h * 8 + 8), slice(start, start + size))]
            rows = rows.astype(F32).reshape(256, size).astype(BF16)
            if p > 0:
                rows = jnp.dot(perm[p - 1], rows, preferred_element_type=F32).astype(BF16)
            begin = h * HALF + STARTS[p] + start
            for i in range(4):
                w = (gw, uw)[i // 2]
                term = jnp.dot(rows, w[i % 2, begin : begin + size, :], preferred_element_type=F32)
                cols = slice(i * UNITS, (i + 1) * UNITS)
                acc[:, cols] = acc[:, cols] + term

    acc[...] = jnp.zeros(acc.shape, F32)

    for p in LATE:
        send_wait(p, 0)
        project(p, 0)
    spread_wait(EARLY, 2, (2, 3, 4, 5))
    for p in EARLY:
        project(p, 0)
    for p in (1, 0):
        send_wait(p, 1)
        project(p, 1)
    for p in range(NP):
        for m in range(6):
            spread(p, 0, m).wait_send()
            spread(p, 1 if p in LATE else 2, m).wait_send()
        for c in range(len(chunks(p))):
            for step in (1, 2, 3):
                send(p, c, step).wait_send()
    for k in range(3):
        for step in (1, 2, 3):
            mix_copy(k, step).wait_send()

    for i in range(2):
        cols = slice(i * UNITS, (i + 1) * UNITS)
        gate = acc[:, cols]
        up = acc[:, 2 * UNITS + i * UNITS : 2 * UNITS + (i + 1) * UNITS]
        inner[0, :, cols] = (gate / (1.0 + jnp.exp(-gate)) * up * wcol[:, 0:1]).astype(BF16)
    for p in range(1, NP):
        inner[p] = lax.dot_general(
            perm[p - 1], inner[0], (((0,), (0,)), ((), ())), preferred_element_type=F32
        ).astype(BF16)

    def expand(p, c):
        start, size = chunks(p)[c]
        halves = []
        for h in range(2):
            begin = h * HALF + STARTS[p] + start
            cols = slice(begin, begin + size)
            value = jnp.dot(inner[p, :, :UNITS], dw[0, :, cols], preferred_element_type=F32)
            value = value + jnp.dot(
                inner[p, :, UNITS:], dw[1, :, cols], preferred_element_type=F32
            )
            halves.append(value.reshape(fin[p].shape[:-2] + (8, size)))
        lead = (slice(None),) * (len(fin[p].shape) - 1)
        fin[p][lead + (slice(start, start + size),)] = jnp.concatenate(
            halves, axis=len(fin[p].shape) - 2
        ).astype(BF16)

    def unsend(p, c, step):
        axis = PARTS[p][0][send_phase(p)]
        start, size = chunks(p)[c]
        other = around(axis, step)
        rest = (slice(None), slice(None), pl.ds(start, size))
        return pltpu.make_async_remote_copy(
            src_ref=fin[p].at[((other,) if p in LATE else (me[X], other)) + rest],
            dst_ref=ret[p].at[(me[axis],) + rest],
            send_sem=un_s.at[p, c, step - 1], recv_sem=un_r.at[p, c, step - 1],
            device_id=device(axis, step), device_id_type=MESH,
        )

    def unsend_own(p):
        axis = PARTS[p][0][send_phase(p)]
        ret[p][me[axis]] = fin[p][(me[axis],) if p in LATE else (me[X], me[axis])]

    def restore(p, c):
        start, size = chunks(p)[c]
        dense = len(dense_axes(p))
        tokens = 8 * 4 ** dense
        for step in (1, 3, 2):
            unsend(p, c, step).wait_recv()
        halves = []
        for h in range(2):
            rows = ret[p][:, :, h * 8 : h * 8 + 8, start : start + size].astype(F32)
            rows = rows.reshape(2 * tokens, size).astype(BF16)
            value = lax.dot_general(
                sels[p][...], rows, (((0,), (0,)), ((), ())), preferred_element_type=F32
            )
            halves.append(value.reshape((4,) * dense + (8, size)))
        lead = (slice(None),) * (dense + 1)
        xb[p][lead + (slice(start, start + size),)] = jnp.concatenate(
            halves, axis=dense
        ).astype(BF16)

    def back(p, k, m):
        axis, lanes = PARTS[p][0][k], PARTS[p][1]
        offset, half, step = ((2, 0, 1), (2, 1, 3), (1, 1, 1), (3, 0, 3), (1, 0, 1), (3, 1, 3))[m]
        start, size = widths(lanes)[half]
        buffer, index = area(p, k, around(axis, offset))
        view = buffer.at[index + (slice(None), pl.ds(start, size))]
        lead = (slice(None),) * k
        if m < 2:
            into = first_in[p].at[(m,) + lead + (slice(None), pl.ds(0, size))]
        else:
            into = last_in[p].at[(m % 2,) + lead + (slice(None), pl.ds(start, size))]
        return pltpu.make_async_remote_copy(
            src_ref=view, dst_ref=into, send_sem=rs_s.at[p, k, m], recv_sem=rs_r.at[p, k, m],
            device_id=device(axis, step), device_id_type=MESH,
        )

    def back_join(p, k):
        axis, lanes = PARTS[p][0][k], PARTS[p][1]
        lead = (slice(None),) * k
        for m in (0, 1):
            back(p, k, m).wait_recv()
            start, size = widths(lanes)[m]
            buffer, index = area(p, k, around(axis, (1, 3)[m]))
            where = index + (slice(None), slice(start, start + size))
            came = first_in[p][(m,) + lead + (slice(None), slice(0, size))]
            buffer[where] = (buffer[where].astype(F32) + came.astype(F32)).astype(BF16)
            back(p, k, 4 + m).start()

    def back_total(p, k):
        axis = PARTS[p][0][k]
        for m in (2, 3, 4, 5):
            back(p, k, m).wait_recv()
        buffer, index = area(p, k, me[axis])
        came = last_in[p]
        total = buffer[index].astype(F32) + came[0].astype(F32) + came[1].astype(F32)
        return total.astype(BF16), buffer, index

    def back_start(p, k):
        for m in range(4):
            back(p, k, m).start()

    def last_copy(p, step):
        axis = PARTS[p][0][0]
        buffer, index = area(p, 0, around(axis, step))
        return pltpu.make_async_remote_copy(
            src_ref=buffer.at[index], dst_ref=final_in[p].at[step - 1],
            send_sem=rs_s.at[p, 0, step], recv_sem=rs_r.at[p, 0, step],
            device_id=device(axis, step), device_id_type=MESH,
        )

    def last_start(p):
        for step in (2, 1, 3):
            last_copy(p, step).start()

    def last_total(p):
        buffer, index = area(p, 0, me[PARTS[p][0][0]])
        total = buffer[index].astype(F32)
        for step in (1, 3, 2):
            last_copy(p, step).wait_recv()
            total = total + final_in[p][step - 1].astype(F32)
        return total.astype(BF16)

    def expand_late(c):
        for p in LATE:
            expand(p, c)
            for step in (2, 1, 3):
                unsend(p, c, step).start()

    fetch[4].wait()
    weights[2].wait()
    expand_late(0)
    for p in EARLY:
        expand(p, 0)
        back_start(p, 2)
    expand_late(1)
    for p in LATE:
        unsend_own(p)
    ring_last(*query_ring)
    ring_end(*query_ring)

    def fact(r, j, i):
        return qg[r // 2, r % 2, j, WIDTH : WIDTH + 16, :].astype(F32)[5:6, i : i + 1]

    entries = [(r, j) for r in range(8) for j in range(2)]

    def migrant(j, carry):
        s = jnp.where(j == 0, slot_a, slot_b)
        to_rank = (dest[s] >> 7).astype(F32)
        to_slot = (dest[s] & 7).astype(F32)
        query = jnp.zeros((QROWS, HEADS), BF16)
        for r, i in entries:
            hit = (fact(r, i, 0) == to_slot) & (to_rank == r)
            query = query + qg[r // 2, r % 2, i] * jnp.where(hit, 1.0, 0.0).astype(BF16)
        tail = query[WIDTH:QROWS].astype(F32)
        tail = jnp.concatenate([tail, jnp.zeros((112, 128), F32)], axis=0).T
        col = jnp.concatenate(
            [tail[:, i : i + 1] for i in range(4)] + [tail[:64, 4:5]], axis=0
        ).astype(BF16)
        n = lengths[s]
        keys = jnp.where(lane == n + 1, col, kt[s])
        scores = jnp.dot(query[:WIDTH].T, keys, preferred_element_type=F32)
        prob, scale = weigh(scores, n + 1)
        result = lax.dot_general(
            prob, keys[:LATENT], (((1,), (1,)), ((), ())), preferred_element_type=F32
        )
        cg[me[0], core, j] = (result * scale).astype(BF16)
        return carry

    lax.fori_loop(0, 2, migrant, 0)
    ring_start(*result_ring)

    for p in EARLY:
        back_join(p, 2)
    for p in LATE:
        restore(p, 0)
        back(p, 1, 0).start()
        back(p, 1, 3).start()
    for p in EARLY:
        total, buffer, index = back_total(p, 2)
        buffer[index] = total
        for step in (2, 1, 3):
            unsend(p, 0, step).start()
        unsend_own(p)
    ring_forward(*result_ring)
    for p in LATE:
        restore(p, 1)
        back(p, 1, 1).start()
        back(p, 1, 2).start()
    for p in LATE:
        back_join(p, 1)
    for p in EARLY:
        restore(p, 0)
        last_start(p)
    for p in LATE:
        total, buffer, index = back_total(p, 1)
        buffer[index] = total
        last_start(p)
    ring_last(*result_ring)
    ring_end(*result_ring)
    for j in range(2):
        s = moving[j]
        mine = s.astype(F32)
        value = jnp.zeros((HEADS, LATENT), BF16)
        for r, i in entries:
            hit = (fact(r, i, 1) == rank.astype(F32)) & (fact(r, i, 2) == mine)
            value = value + cg[r // 2, r % 2, i] * jnp.where(hit, 1.0, 0.0).astype(BF16)
        for t in range(SLOTS):
            c2[t] = jnp.where(s == t, value, c2[t])
    pltpu.make_async_copy(c2, out2, o2_sem).start()
    for p in EARLY + LATE:
        total = last_total(p)
        lanes = PARTS[p][1]
        for h in range(2):
            cols = slice(h * HALF + STARTS[p], h * HALF + STARTS[p] + lanes)
            routed[:, cols] = total[h * 8 : h * 8 + 8]
    for p in range(NP):
        for m in range(6):
            back(p, 1 if p in LATE else 2, m).wait_send()
        for step in (1, 2, 3):
            last_copy(p, step).wait_send()
        for c in range(len(chunks(p))):
            for step in (1, 2, 3):
                unsend(p, c, step).wait_send()
    for s in range(SLOTS):
        out_copy(s).wait()
    pltpu.make_async_copy(c2, out2, o2_sem).wait()


def finish(first, second, tokens, out1, out2, routed, held, sem_in, sem_out):
    pairs = [(i, s) for i in range(2) for s in range(0, SLOTS, 2)]
    sources, targets = (first, second), (out1, out2)

    def inward(i, s):
        return pltpu.make_async_copy(
            sources[i].at[pl.ds(s, 2)], held.at[i, pl.ds(s, 2)], sem_in.at[i, s]
        )

    def outward(i, s):
        return pltpu.make_async_copy(
            held.at[i, pl.ds(s, 2)], targets[i].at[pl.ds(s, 2)], sem_out.at[i, s]
        )

    for pair in pairs:
        inward(*pair).start()
    routed[...] = tokens[...]
    for pair in pairs:
        inward(*pair).wait()
        outward(*pair).start()
    for pair in pairs:
        outward(*pair).wait()


def shards(
    latent_cache, context_lengths, destination, query_first, latent_first, query_second,
    latent_second, hidden, expert_ids, gate_weights, expert_gate, expert_up, expert_down,
):
    anywhere = pl.BlockSpec(memory_space=pl.ANY)
    vmem = pl.BlockSpec(memory_space=pltpu.VMEM)
    smem = pl.BlockSpec(memory_space=pltpu.SMEM)

    def each(shape):
        return [pltpu.VMEM(shape(p, PARTS[p][1]), BF16) for p in range(NP)]

    def groups(p):
        return 8 if p in LATE else 2

    def ring_lead(p):
        return (4,) if p in LATE else (4, 2)

    buffers = (
        each(lambda p, lanes: (4,) * len(dense_axes(p)) + (16, lanes))
        + each(lambda p, lanes: (4, groups(p), 16, lanes))
        + each(lambda p, lanes: (4, 8, 16, lanes) if p in LATE else (4, 4, 2, 16, lanes))
        + each(lambda p, lanes: (4, groups(p), 16, lanes))
        + each(lambda p, lanes: (32 * groups(p), 16 * groups(p)))
        + each(lambda p, lanes: (2,) + ring_lead(p) + (16, widths(lanes)[0][1]))
        + each(lambda p, lanes: (3, 16, lanes))
        + each(lambda p, lanes: (2,) + ring_lead(p) + (16, lanes))
    )
    dma = pltpu.SemaphoreType.DMA
    shapes = (
        jax.ShapeDtypeStruct((SLOTS, HEADS, LATENT), BF16),
        jax.ShapeDtypeStruct((SLOTS, HEADS, LATENT), BF16),
        jax.ShapeDtypeStruct((SLOTS, D), BF16),
    )
    results = pl.pallas_call(
        kernel,
        out_shape=shapes,
        in_specs=[smem, smem] + [anywhere] * 3 + [vmem] * 5 + [anywhere] * 3,
        out_specs=(anywhere, anywhere, vmem),
        scratch_shapes=[
            pltpu.VMEM((SLOTS, WIDTH, CONTEXT), BF16),
            pltpu.VMEM((SLOTS, WIDTH, HEADS), BF16),
            pltpu.VMEM((SLOTS, WIDTH, HEADS), BF16),
            pltpu.VMEM((SLOTS, HEADS, LATENT), BF16),
            pltpu.VMEM((SLOTS, HEADS, LATENT), BF16),
            pltpu.VMEM((4, 2, 2, QROWS, HEADS), BF16),
            pltpu.VMEM((4, 2, 2, HEADS, LATENT), BF16),
            pltpu.VMEM((2, D, UNITS), BF16),
            pltpu.VMEM((2, D, UNITS), BF16),
            pltpu.VMEM((2, UNITS, D), BF16),
            pltpu.VMEM((256, 4 * UNITS), F32),
            pltpu.VMEM((WIDTH, 128), F32),
            pltpu.VMEM((4, 4, 4, SLOTS, 128), F32),
            pltpu.VMEM((3, 256, 256), BF16),
            pltpu.VMEM((NP, 256, 2 * UNITS), BF16),
            pltpu.VMEM((256, 128), F32),
        ]
        + buffers
        + [
            dma((NP, 3, 6)), dma((NP, 3, 6)), dma((NP, 3, 6)), dma((NP, 3, 6)),
            dma((NP, 2, 3)), dma((NP, 2, 3)), dma((NP, 2, 3)), dma((NP, 2, 3)),
            dma((3, 3)), dma((3, 3)),
            dma((10,)), dma((10,)), dma((10,)), dma((10,)), dma((3,)), dma((3,)),
            dma((SLOTS,)), dma((5,)), dma((SLOTS,)), dma,
        ],
        compiler_params=pltpu.CompilerParams(
            collective_id=0, has_side_effects=True, vmem_limit_bytes=64 * 1024 * 1024 - 65536
        ),
    )(
        context_lengths, destination,
        jnp.swapaxes(latent_cache, 1, 2), jnp.swapaxes(query_first, 1, 2),
        jnp.swapaxes(query_second, 1, 2), latent_first, latent_second, hidden,
        expert_ids.T, gate_weights.T, expert_gate, expert_up, expert_down,
    )
    return pl.pallas_call(
        finish,
        out_shape=shapes,
        in_specs=[anywhere, anywhere, vmem],
        out_specs=(anywhere, anywhere, vmem),
        scratch_shapes=[
            pltpu.VMEM((2, SLOTS, HEADS, LATENT), BF16), dma((2, SLOTS)), dma((2, SLOTS)),
        ],
    )(*results)


def solution(mesh):
    rows = P(("req", "exp"), None)
    cubes = P(("req", "exp"), None, None)
    flat = P(("req", "exp"))
    return jax.shard_map(
        shards,
        mesh=mesh,
        in_specs=(
            cubes, flat, flat, cubes, rows, cubes, rows, rows, rows, rows,
            P("exp", None, "req"), P("exp", None, "req"), P("exp", "req", None),
        ),
        out_specs=(cubes, cubes, rows),
        check_vma=False,
    )
```
